128 devices in a mesh: dp: 32 (over z_lo, y, x), tensor: 4 (over z_hi, core).
Axes of the slice: x: 4, y: 4, z: 4 (z_hi: 2, z_lo: 2; z = z_hi * 2 + z_lo), core: 2. Of those that a mesh axis runs over, the one named last changes fastest.
Arguments:
- tokens: bfloat16 [16384, 1536], P(('dp', 'tensor')), may hold values from -6 to 6
- norm_gain: float32 [2, 2, 1536], replicated, may hold values from 0.1 to 1.9
- norm_shift: float32 [2, 2, 1536], replicated, may hold values from -3 to 3
- w_qkv: bfloat16 [2, 1536, 3, 1536], P(None, None, None, 'tensor'), may hold values from -0.15625 to 0.15625
- w_out: bfloat16 [2, 1536, 1536], P(None, 'tensor'), may hold values from -1.25 to 1.25
- w_up: bfloat16 [2, 1536, 6144], P(None, None, 'tensor'), may hold values from -0.15625 to 0.15625
- w_down: bfloat16 [2, 6144, 1536], P(None, 'tensor'), may hold values from -0.109375 to 0.109375
- granularity: int32 [32, 1], P('dp'), may hold values from 0 to 3
- cotangent: bfloat16 [16384, 1536], P(('dp', 'tensor')), may hold values from -24 to 24
Outputs:
- activations: bfloat16 [16384, 1536], P(('dp', 'tensor'))
- input_grad: float32 [16384, 1536], P(('dp', 'tensor'))
- grad_qkv: float32 [2, 1536, 3, 1536], P(None, 'dp', None, 'tensor')
- grad_out: float32 [2, 1536, 1536], P(None, 'tensor', 'dp')
- grad_up: float32 [2, 1536, 6144], P(None, 'dp', 'tensor')
- grad_down: float32 [2, 6144, 1536], P(None, 'tensor', 'dp')
- grad_gain: float32 [2, 2, 1536], replicated
- grad_shift: float32 [2, 2, 1536], replicated
- ffn_shift_grad: float32 [2, 1536], replicated
The draws below stay inside these ranges and needn't reach their ends.
Inputs may be any that keep to these rules, and one draw needn't show every extreme that they name: Every granularity index 0, 1, 2 and 3 is given to some sequence.
All inputs are finite; a program needn't handle non-finite values.
Results may differ from the reference program's by a relative error of at most 0.035.
Values may be sent and summed in bfloat16 or wider, within the bound.
No kernel may reach another device: no remote copies, remote signals or barrier semaphores. Data moves between devices by JAX's collectives and lax.ppermute only.
A program may use at most 192 MiB of HBM per device.

```python
import jax
import jax.numpy as jnp
from jax import lax

D = 1536
HEADS = 12
HEAD_SIZE = 128
FF = 6144
LAYERS = 2
SEQ_LEN = 512
TOKENS = 16384
HID = 1536
N_DP = 32


def raised(array, rng, source, target, shards_of, factor):
    owner, partner = [(jnp.arange(array.shape[dim]) // (array.shape[dim] // shards_of)).reshape([-1 if axis == dim else 1 for axis in range(array.ndim)]) for dim in (source, target)]
    chosen = jax.random.permutation(rng, shards_of)[partner]
    strong = (owner == chosen) | (owner == (partner + shards_of // 2) % shards_of)
    return jnp.where(strong, factor * array, array)


def shard_levels(rng, dims, pieces, smallest, high):
    level = 1.0
    for dim, shards_of in pieces:
        draws = jax.random.uniform(jax.random.fold_in(jax.random.fold_in(rng, 6), dim), (shards_of,), jnp.float32, smallest / len(pieces), high / len(pieces))
        level = level * jnp.repeat(jnp.exp(draws), dims[dim] // shards_of).reshape((-1,) + (1,) * (len(dims) - 1 - dim))
    return level


def different_ones(rng, rows, number_of, top, lift):
    sequence = jax.random.permutation(jax.random.fold_in(rng, 1), number_of)
    pull = sequence
    for power in range(3):
        pull = pull * pull // number_of
    pull = pull * lift // number_of
    lots = jax.random.randint(jax.random.fold_in(rng, 2), (rows, number_of), 0, 4096) + pull
    fixed_rows = jax.random.permutation(jax.random.fold_in(rng, 3), rows)[jnp.arange(number_of) % rows]
    lots = jnp.where(jnp.arange(rows)[:, None] == fixed_rows[None, :], 1 << 14, lots)
    priority = lots * number_of + jnp.arange(number_of)
    return lax.top_k(priority.astype(jnp.int32), top)[1].astype(jnp.int32)


def normal_values(key, dims, spread, most, pieces=(), kind=jnp.bfloat16):
    drawn = jax.random.normal(key, dims, jnp.float32) * spread
    if len(pieces) > 0:
        drawn = shard_levels(key, dims, pieces, -0.22, 0.18) * drawn
    return jnp.clip(drawn, min=-most, max=most).astype(kind)


def noise_with(own_key, dims, width, most, shards, heavy, held_as=jnp.bfloat16):
    drawn = width * jax.random.normal(own_key, dims, jnp.float32)
    if shards:
        drawn = drawn * shard_levels(own_key, dims, shards, -0.22, 0.18)
    return jnp.clip(raised(drawn, jax.random.fold_in(own_key, 3), *heavy), -most, most).astype(held_as)


def setup_inputs(seed: int = 0) -> dict:
    splits = jax.random.split(jax.random.key(seed), 10)
    return {
        "tokens": normal_values(splits[0], (TOKENS, D), 1.0, 6.0, ((0, 128),)),
        "norm_gain": jnp.clip(1.0 + 0.18 * jax.random.normal(splits[1], (LAYERS, 2, D), jnp.float32), 0.1, 1.9),
        "norm_shift": normal_values(splits[2], (LAYERS, 2, D), 0.5, 3.0, (), jnp.float32),
        "w_qkv": normal_values(splits[3], (LAYERS, D, 3, HID), D ** -0.5, 0.15625, ((3, 4),)),
        "w_out": normal_values(splits[4], (LAYERS, HID, D), (max(HEADS * HEAD_SIZE // 64, 4)) ** -0.5, 1.25, ((1, 4),)),
        "w_up": normal_values(splits[5], (LAYERS, D, FF), D ** -0.5, 0.15625, ((2, 4),)),
        "w_down": normal_values(splits[6], (LAYERS, FF, D), (FF // 2) ** -0.5, 0.109375, ((1, 4),)),
        "granularity": different_ones(splits[7], N_DP, 4, 1, 2048),
        "cotangent": noise_with(splits[8], (TOKENS, D), 1.0, 24.0, ((0, 128),), (0, 1, 128, 5.5)),
    }


norm_epsilon = 1e-05
rotary_base = 10000.0
masked_score = -1e+30
highest = lax.Precision.HIGHEST

@jax.custom_vjp
def low(v):
    return lax.optimization_barrier(v.astype(jnp.bfloat16)).astype(jnp.float32)

@jax.custom_vjp
def low_back(v):
    return v

def low_keep(v):
    return (low(v), None)

def low_pass(kept, grad):
    return (grad,)

def back_keep(v):
    return (v, None)

def back_low(kept, grad):
    return (low(grad),)
low.defvjp(low_keep, low_pass)
low_back.defvjp(back_keep, back_low)

def layer_norm(values, gain_row, shift_row):
    centered = values - lax.optimization_barrier(jnp.mean(values, axis=-1, keepdims=True))
    variance = lax.optimization_barrier(jnp.mean(centered * centered, axis=-1, keepdims=True))
    return centered * lax.rsqrt(variance + norm_epsilon) * gain_row + shift_row

def rotary_tables(length, head_size):
    half_size = head_size // 2
    places = jnp.arange(length, dtype=jnp.float32)[:, None]
    frequency = rotary_base ** (-jnp.arange(half_size, dtype=jnp.float32) / half_size)
    angles = places * frequency[None, :]
    return (jnp.cos(angles)[:, None, :], jnp.sin(angles)[:, None, :])

def rotate(values, cosine_table, sine_table):
    half_size = values.shape[-1] // 2
    first_half = values[..., :half_size]
    second_half = values[..., half_size:]
    return jnp.concatenate([first_half * cosine_table - second_half * sine_table, second_half * cosine_table + first_half * sine_table], axis=-1)

def matmul(left_side, right_side):
    return jnp.dot(left_side, right_side, precision=highest, preferred_element_type=jnp.float32)

def sublayers(stream, norm_gains, norm_shifts, qkv_weight, out_weight, up_weight, down_weight, prefix_width):
    length = stream.shape[0]
    cosine_table, sine_table = rotary_tables(length, HEAD_SIZE)
    head_shape = (length, HEADS, HEAD_SIZE)
    normed = low(layer_norm(stream, norm_gains[0], norm_shifts[0]))
    projected = jnp.einsum('td,dch->tch', normed, qkv_weight, precision=highest)
    queries = low(rotate(low_back(projected[:, 0]).reshape(head_shape), cosine_table, sine_table) * HEAD_SIZE ** (-0.5))
    key_rows = low(rotate(low_back(projected[:, 1]).reshape(head_shape), cosine_table, sine_table))
    value_rows = low(low_back(projected[:, 2])).reshape(head_shape)
    scores = low_back(jnp.einsum('qhe,khe->hqk', queries, key_rows, precision=highest))
    places = jnp.arange(length, dtype=jnp.int32)
    allowed = places[None, :] <= places[:, None]
    probability = low(jax.nn.softmax(jnp.where(allowed[None], scores, masked_score), axis=-1))
    mixture = low(low_back(jnp.einsum('hqk,khe->qhe', probability, value_rows, precision=highest)))
    mixture = mixture.reshape(length, HEADS * HEAD_SIZE)
    middle = stream + low_back(matmul(mixture, out_weight))
    normed_two = low(layer_norm(middle, norm_gains[1], norm_shifts[1]))
    upward = low_back(matmul(normed_two, up_weight))
    keep_mask = (jnp.arange(FF, dtype=jnp.int32) < prefix_width).astype(jnp.float32)
    hidden = low(jax.nn.gelu(upward, approximate=True) * keep_mask)
    return middle + low_back(matmul(hidden, down_weight))

def forward(stream, params, prefix_width):
    gain_table, shift_table, qkv_table, out_table, up_table, down_table = params
    for layer_index in range(LAYERS):
        stream = sublayers(stream, gain_table[layer_index], shift_table[layer_index], qkv_table[layer_index], out_table[layer_index], up_table[layer_index], down_table[layer_index], prefix_width)
    return stream

def reference(tokens, norm_gain, norm_shift, w_qkv, w_out, w_up, w_down, granularity, cotangent):
    params = (norm_gain.astype(jnp.float32), norm_shift.astype(jnp.float32), w_qkv.astype(jnp.float32), w_out.astype(jnp.float32), w_up.astype(jnp.float32), w_down.astype(jnp.float32))
    sequence_rows = tokens.astype(jnp.float32).reshape(N_DP, SEQ_LEN, D)
    sequence_cotangent = cotangent.astype(jnp.float32).reshape(N_DP, SEQ_LEN, D)
    prefix_widths = FF // 8 * 2 ** granularity[:, 0]

    def sequence_step(totals, entries):
        rows_input, rows_cotangent, prefix_width = entries

        def run_layers(stream, weights):
            return forward(stream, weights, prefix_width)
        outcome, pullback = jax.vjp(run_layers, rows_input, params)
        input_gradient, weight_gradients = pullback(rows_cotangent)
        return (jax.tree.map(jnp.add, totals, weight_gradients), (outcome, input_gradient))
    initial = jax.tree.map(jnp.zeros_like, params)
    totals, (outcomes, input_gradients) = lax.scan(sequence_step, initial, (sequence_rows, sequence_cotangent, prefix_widths))
    return (outcomes.reshape(TOKENS, D).astype(jnp.bfloat16), input_gradients.reshape(TOKENS, D), totals[2], totals[3], totals[4], totals[5], totals[0], totals[1], totals[1][:, 1, :])
```

```python
import functools
import itertools

import jax
import jax.numpy as jnp
from jax import lax
from jax.experimental import pallas as pl
from jax.experimental.pallas import tpu as pltpu
from jax.sharding import Mesh
from jax.sharding import PartitionSpec as P

D = 1536
FF = 6144
E = 128
HEADS = 3
HID = HEADS * E
SLICE = 1536
HALF = 256
OWN = 128
FB = 384
EPS = 1e-5
BASE = 10000.0
MASKED = -1e30
SCALE = E**-0.5
C1 = 0.7978845608028654
C2 = 0.044715

AXES = ("zl", "y", "x", "zh", "c")
SIZES = (2, 4, 4, 2, 2)
F32 = jnp.float32
BF16 = jnp.bfloat16


def flat(place):
    index = 0
    for size, at in zip(SIZES, place):
        index = index * size + at
    return index


def pairs(move):
    return [
        (flat(p), flat(move(*p))) for p in itertools.product(*[range(s) for s in SIZES])
    ]


CORE = pairs(lambda zl, y, x, zh, c: (zl, y, x, zh, 1 - c))
FAR = pairs(lambda zl, y, x, zh, c: (zl, y, x, 1 - zh, c))
ZLO = pairs(lambda zl, y, x, zh, c: (1 - zl, y, x, zh, c))


def x_by(d):
    return pairs(lambda zl, y, x, zh, c: (zl, y, (x + d) % 4, zh, c))


def y_by(d):
    return pairs(lambda zl, y, x, zh, c: (zl, (y + d) % 4, x, zh, c))


def x_flip(d):
    return pairs(lambda zl, y, x, zh, c: (zl, y, x ^ d, zh, c))


def y_flip(d):
    return pairs(lambda zl, y, x, zh, c: (zl, y ^ d, x, zh, c))


def send(values, perm):
    return lax.ppermute(values, AXES, perm)


def dot(a, b):
    return jnp.dot(a, b, preferred_element_type=F32)


def dot_t(a, b):
    return lax.dot_general(a, b, (((1,), (1,)), ((), ())), preferred_element_type=F32)


def t_dot(a, b):
    return lax.dot_general(a, b, (((0,), (0,)), ((), ())), preferred_element_type=F32)


def params(mb):
    return pltpu.CompilerParams(vmem_limit_bytes=mb * 1024 * 1024)


def cost(flops, size, trans=0):
    return pl.CostEstimate(flops=int(flops), bytes_accessed=int(size), transcendentals=int(trans))


def whole(shape):
    zeros = (0,) * len(shape)
    return pl.BlockSpec(shape, lambda *_: zeros)


SMEM = pl.BlockSpec(memory_space=pltpu.SMEM)


def moments(x):
    mean = jnp.mean(x, axis=-1, keepdims=True)
    centered = x - mean
    var = jnp.mean(centered * centered, axis=-1, keepdims=True)
    return centered, lax.rsqrt(var + EPS)


def norm_kernel(x_ref, g_ref, b_ref, a_ref):
    centered, r = moments(x_ref[...].astype(F32))
    a_ref[...] = (centered * r * g_ref[...] + b_ref[...]).astype(BF16)


def norm(x, gain, shift):
    rows = x.shape[0]
    return pl.pallas_call(
        norm_kernel,
        out_shape=jax.ShapeDtypeStruct((rows, D), BF16),
        in_specs=[whole((rows, D)), whole((1, D)), whole((1, D))],
        out_specs=whole((rows, D)),
        grid=(1,),
        compiler_params=params(16),
        cost_estimate=cost(10 * rows * D, 6 * rows * D),
        name="norm",
    )(x, gain, shift)


def add_norm_kernel(x_ref, s_ref, r_ref, g_ref, b_ref, m_ref, a_ref):
    x = x_ref[...].astype(F32) + (s_ref[...].astype(F32) + r_ref[...].astype(F32))
    m_ref[...] = x
    centered, r = moments(x)
    a_ref[...] = (centered * r * g_ref[...] + b_ref[...]).astype(BF16)


def add_norm(x, s, r, gain, shift):
    rows = x.shape[0]
    return pl.pallas_call(
        add_norm_kernel,
        out_shape=(
            jax.ShapeDtypeStruct((rows, D), F32),
            jax.ShapeDtypeStruct((rows, D), BF16),
        ),
        in_specs=[whole((rows, D))] * 3 + [whole((1, D))] * 2,
        out_specs=(whole((rows, D)), whole((rows, D))),
        grid=(1,),
        compiler_params=params(16),
        cost_estimate=cost(10 * rows * D, 14 * rows * D),
        name="add_norm",
    )(x, s, r, gain, shift)


def norm_back_kernel(x0_ref, x1_ref, s_ref, r_ref, prev_ref, g_ref, d_ref, low_ref, sums_ref):
    x = jnp.concatenate([x0_ref[...], x1_ref[...]], axis=0).astype(F32)
    da = s_ref[...].astype(F32) + r_ref[...].astype(F32)
    centered, r = moments(x)
    xh = centered * r
    e = da * g_ref[...]
    mean_e = jnp.mean(e, axis=-1, keepdims=True)
    mean_ex = jnp.mean(e * xh, axis=-1, keepdims=True)
    out = prev_ref[...].astype(F32) + r * (e - mean_e - xh * mean_ex)
    d_ref[...] = out
    low_ref[...] = out.astype(BF16)
    sums_ref[0:1, :] = jnp.sum(da * xh, axis=0, keepdims=True)
    sums_ref[1:2, :] = jnp.sum(da, axis=0, keepdims=True)


def norm_back(x0, x1, s, r, prev, gain):
    rows = 2 * OWN
    return pl.pallas_call(
        norm_back_kernel,
        out_shape=(
            jax.ShapeDtypeStruct((rows, D), F32),
            jax.ShapeDtypeStruct((rows, D), BF16),
            jax.ShapeDtypeStruct((2, D), F32),
        ),
        in_specs=[whole((OWN, D))] * 2 + [whole((rows, D))] * 3 + [whole((1, D))],
        out_specs=(whole((rows, D)), whole((rows, D)), whole((2, D))),
        grid=(1,),
        compiler_params=params(32),
        cost_estimate=cost(20 * rows * D, 18 * rows * D),
        name="norm_back",
    )(x0, x1, s, r, prev, gain)


def rot(x, cos, sin):
    return x * cos + pltpu.roll(x, E // 2, 1) * sin


def allowed(core, q_start, rows, k_start, columns):
    flip = core * OWN
    q = (lax.broadcasted_iota(jnp.int32, (rows, columns), 0) + q_start) ^ flip
    k = (lax.broadcasted_iota(jnp.int32, (rows, columns), 1) + k_start) ^ flip
    return k <= q


def softmax(s):
    top = jnp.max(s, axis=-1, keepdims=True)
    e = jnp.exp(s - top)
    return e / jnp.sum(e, axis=-1, keepdims=True)


def attend_kernel(chunk, core_ref, am_ref, at_ref, w_ref, wo_ref, cos_ref, sin_ref, *rest):
    if chunk:
        before_ref, qkv_ref, o_ref, pm_ref, pt_ref, acc = rest
    else:
        qkv_ref, o_ref, pm_ref, pt_ref, acc = rest
    step = pl.program_id(0)
    a = jnp.concatenate([am_ref[...], at_ref[...]], axis=0)
    w = jnp.concatenate([w_ref[0, 0], w_ref[0, 1], w_ref[0, 2]], axis=1)
    p = dot(a, w)
    cos, sin = cos_ref[...], sin_ref[...]
    q = (rot(p[:, :E], cos, sin) * SCALE).astype(BF16)
    k = rot(p[:, E : 2 * E], cos, sin).astype(BF16)
    v = p[:, 2 * E :].astype(BF16)
    qkv_ref[0], qkv_ref[1], qkv_ref[2] = q, k, v
    if chunk:
        k = jnp.concatenate([before_ref[1], k], axis=0)
        v = jnp.concatenate([before_ref[2], v], axis=0)
    s = dot_t(q, k)
    s = jnp.where(allowed(core_ref[0], chunk * HALF, HALF, 0, s.shape[1]), s, MASKED)
    o = dot(softmax(s).astype(BF16), v).astype(BF16)
    o_ref[...] = o
    part = dot(o, wo_ref[0])

    @pl.when(step == 0)
    def _():
        acc[...] = part

    @pl.when(step == 1)
    def _():
        acc[...] += part

    @pl.when(step == HEADS - 1)
    def _():
        total = acc[...] + part
        pm_ref[...] = total[:OWN].astype(BF16)
        pt_ref[...] = total[OWN:].astype(BF16)


def attend(layer, chunk, core, am, at, w_qkv, w_out, cos, sin, before):
    head = pl.BlockSpec((3, HALF, E), lambda h: (0, 0, h))
    tables = pl.BlockSpec((HALF, E), lambda h: (chunk, 0))
    piece = whole((OWN, D))
    return pl.pallas_call(
        functools.partial(attend_kernel, chunk),
        out_shape=(
            jax.ShapeDtypeStruct((3, HALF, HID), BF16),
            jax.ShapeDtypeStruct((HALF, HID), BF16),
            jax.ShapeDtypeStruct((OWN, D), BF16),
            jax.ShapeDtypeStruct((OWN, D), BF16),
        ),
        in_specs=[
            SMEM,
            am[1],
            at[1],
            pl.BlockSpec((1, 3, D, E), lambda h: (layer, 0, 0, h)),
            pl.BlockSpec((1, E, D), lambda h: (layer, h, 0)),
            tables,
            tables,
        ]
        + ([head] if chunk else []),
        out_specs=(head, pl.BlockSpec((HALF, E), lambda h: (0, h)), piece, piece),
        scratch_shapes=[pltpu.VMEM((HALF, D), F32)],
        grid=(HEADS,),
        compiler_params=params(32),
        cost_estimate=cost(2 * HALF * D * 4 * HID, 2 * 4 * HID * D + 8 * HALF * D),
        name="attend",
    )(core, am[0], at[0], w_qkv, w_out, cos, sin, *([before] if chunk else []))


def attend_back_kernel(
    core_ref, gm_ref, gt_ref, w_ref, wo_ref, cos_ref, sin_ref, c0_ref, c1_ref, d_ref, pm_ref, pt_ref, acc
):
    step = pl.program_id(0)
    g0 = jnp.concatenate([gm_ref[:OWN], gt_ref[:OWN]], axis=0)
    g1 = jnp.concatenate([gm_ref[OWN:], gt_ref[OWN:]], axis=0)
    do0 = dot_t(g0, wo_ref[0]).astype(BF16)
    do1 = dot_t(g1, wo_ref[0]).astype(BF16)
    k = jnp.concatenate([c0_ref[1], c1_ref[1]], axis=0)
    v = jnp.concatenate([c0_ref[2], c1_ref[2]], axis=0)
    core = core_ref[0]

    def block(chunk, q, do, keys, values):
        s = dot_t(q, keys)
        s = jnp.where(allowed(core, chunk * HALF, HALF, 0, s.shape[1]), s, MASKED)
        prob = softmax(s)
        dp = dot_t(do, values)
        ds = (prob * (dp - jnp.sum(prob * dp, axis=-1, keepdims=True))).astype(BF16)
        return dot(ds, keys), t_dot(ds, q), t_dot(prob.astype(BF16), do)

    dq1, dk1, dv1 = block(1, c1_ref[0], do1, k, v)
    dq0, dk0, dv0 = block(0, c0_ref[0], do0, c0_ref[1], c0_ref[2])
    cos, sin = cos_ref[...], -sin_ref[...]
    dq = (rot(jnp.concatenate([dq0, dq1], axis=0), cos, sin) * SCALE).astype(BF16)
    dk = jnp.concatenate([dk0 + dk1[:HALF], dk1[HALF:]], axis=0)
    dk = rot(dk, cos, sin).astype(BF16)
    dv = jnp.concatenate([dv0 + dv1[:HALF], dv1[HALF:]], axis=0).astype(BF16)
    d_ref[0], d_ref[1], d_ref[2] = dq, dk, dv
    w = jnp.concatenate([w_ref[0, 0], w_ref[0, 1], w_ref[0, 2]], axis=1)
    part = dot_t(jnp.concatenate([dq, dk, dv], axis=1), w)

    @pl.when(step == 0)
    def _():
        acc[...] = part

    @pl.when(step == 1)
    def _():
        acc[...] += part

    @pl.when(step == HEADS - 1)
    def _():
        total = acc[...] + part
        split_rows(total, pm_ref, pt_ref)


def split_rows(total, pm_ref, pt_ref):
    pm_ref[:OWN] = total[:OWN].astype(BF16)
    pt_ref[:OWN] = total[OWN : 2 * OWN].astype(BF16)
    pm_ref[OWN:] = total[2 * OWN : 3 * OWN].astype(BF16)
    pt_ref[OWN:] = total[3 * OWN :].astype(BF16)


def attend_back(layer, core, gm, gt, w_qkv, w_out, cos, sin, saved0, saved1):
    rows = 2 * HALF
    head = pl.BlockSpec((3, HALF, E), lambda h: (0, 0, h))
    piece = whole((HALF, D))
    return pl.pallas_call(
        attend_back_kernel,
        out_shape=(
            jax.ShapeDtypeStruct((3, rows, HID), BF16),
            jax.ShapeDtypeStruct((HALF, D), BF16),
            jax.ShapeDtypeStruct((HALF, D), BF16),
        ),
        in_specs=[
            SMEM,
            piece,
            piece,
            pl.BlockSpec((1, 3, D, E), lambda h: (layer, 0, 0, h)),
            pl.BlockSpec((1, E, D), lambda h: (layer, h, 0)),
            whole((rows, E)),
            whole((rows, E)),
            head,
            head,
        ],
        out_specs=(pl.BlockSpec((3, rows, E), lambda h: (0, 0, h)), piece, piece),
        scratch_shapes=[pltpu.VMEM((rows, D), F32)],
        grid=(HEADS,),
        compiler_params=params(40),
        cost_estimate=cost(2 * rows * D * 5 * HID, 2 * 4 * HID * D + 8 * rows * D),
        name="attend_back",
    )(core, gm, gt, w_qkv, w_out, cos, sin, saved0, saved1)


def feed_kernel(width_ref, am_ref, at_ref, up_ref, down_ref, hid_ref, slope_ref, pm_ref, pt_ref, acc):
    step = pl.program_id(0)
    a = jnp.concatenate([am_ref[...], at_ref[...]], axis=0)
    u = dot(a, up_ref[0])
    place = lax.broadcasted_iota(jnp.int32, u.shape, 1) + step * FB
    keep = place < width_ref[0]
    square = u * u
    t = jnp.tanh(C1 * (u + C2 * u * square))
    hid = jnp.where(keep, 0.5 * u * (1.0 + t), 0.0).astype(BF16)
    slope = 0.5 * (1.0 + t) + 0.5 * u * (1.0 - t * t) * (C1 * (1.0 + 3.0 * C2 * square))
    slope_ref[...] = jnp.where(keep, slope, 0.0).astype(BF16)
    hid_ref[...] = hid
    part = dot(hid, down_ref[0])

    @pl.when(step == 0)
    def _():
        acc[...] = part

    @pl.when(step > 0)
    def _():
        acc[...] += part

    @pl.when(step == SLICE // FB - 1)
    def _():
        pm_ref[...] = acc[:OWN].astype(BF16)
        pt_ref[...] = acc[OWN:].astype(BF16)


def feed(layer, width, am, at, w_up, w_down):
    piece = whole((OWN, D))
    block = pl.BlockSpec((HALF, FB), lambda j: (0, j))
    return pl.pallas_call(
        feed_kernel,
        out_shape=(
            jax.ShapeDtypeStruct((HALF, SLICE), BF16),
            jax.ShapeDtypeStruct((HALF, SLICE), BF16),
            jax.ShapeDtypeStruct((OWN, D), BF16),
            jax.ShapeDtypeStruct((OWN, D), BF16),
        ),
        in_specs=[
            SMEM,
            piece,
            piece,
            pl.BlockSpec((1, D, FB), lambda j: (layer, 0, j)),
            pl.BlockSpec((1, FB, D), lambda j: (layer, j, 0)),
        ],
        out_specs=(block, block, piece, piece),
        scratch_shapes=[pltpu.VMEM((HALF, D), F32)],
        grid=(SLICE // FB,),
        compiler_params=params(32),
        cost_estimate=cost(4 * HALF * D * SLICE, 4 * SLICE * D + 8 * HALF * D),
        name="feed",
    )(width, am, at, w_up, w_down)


def feed_back_kernel(gm_ref, gt_ref, down_ref, up_ref, slope0_ref, slope1_ref, du_ref, pm_ref, pt_ref, acc):
    step = pl.program_id(0)
    g = jnp.concatenate([gm_ref[:OWN], gt_ref[:OWN], gm_ref[OWN:], gt_ref[OWN:]], axis=0)
    dhid = dot_t(g, down_ref[0])
    slope = jnp.concatenate([slope0_ref[...], slope1_ref[...]], axis=0).astype(F32)
    du = (dhid * slope).astype(BF16)
    du_ref[...] = du
    part = dot_t(du, up_ref[0])

    @pl.when(step == 0)
    def _():
        acc[...] = part

    @pl.when(step > 0)
    def _():
        acc[...] += part

    @pl.when(step == SLICE // FB - 1)
    def _():
        split_rows(acc[...], pm_ref, pt_ref)


def feed_back(layer, gm, gt, w_up, w_down, slope0, slope1):
    rows = 2 * HALF
    piece = whole((HALF, D))
    block = pl.BlockSpec((HALF, FB), lambda j: (0, j))
    return pl.pallas_call(
        feed_back_kernel,
        out_shape=(
            jax.ShapeDtypeStruct((rows, SLICE), BF16),
            jax.ShapeDtypeStruct((HALF, D), BF16),
            jax.ShapeDtypeStruct((HALF, D), BF16),
        ),
        in_specs=[
            piece,
            piece,
            pl.BlockSpec((1, FB, D), lambda j: (layer, j, 0)),
            pl.BlockSpec((1, D, FB), lambda j: (layer, 0, j)),
            block,
            block,
        ],
        out_specs=(pl.BlockSpec((rows, FB), lambda j: (0, j)), piece, piece),
        scratch_shapes=[pltpu.VMEM((rows, D), F32)],
        grid=(SLICE // FB,),
        compiler_params=params(40),
        cost_estimate=cost(4 * rows * D * SLICE, 4 * SLICE * D + 8 * rows * D),
        name="feed_back",
    )(gm, gt, w_down, w_up, slope0, slope1)


NB = 384


def rows_of(first, d, place_ref):
    at = lax.rem(place_ref[0 if first else 1] + d, 4)
    offsets = []
    for major in range(2):
        for minor in range(4):
            block = (major * 4 + minor) * 4 + at if first else (major * 4 + at) * 4 + minor
            offsets.append(pl.multiple_of(block * 48, 16))
    return offsets


def assemble(refs):
    if len(refs) == 2:
        m, t = refs
        return [m[:OWN], t[:OWN], m[OWN:], t[OWN:]]
    return [r[...] for r in refs]


def grad_kernel(first, counts, steps, place_ref, *refs):
    lefts, refs = refs[: sum(counts)], refs[sum(counts) :]
    count = len(steps)
    rights, refs = refs[: sum(n for n, _ in steps)], refs[sum(n for n, _ in steps) :]
    outs, (turned, total) = refs[:4], refs[4:]
    step = pl.program_id(0)
    start = 0
    at_left = at_right = 0
    for number in range(count):
        left = lefts[at_left : at_left + counts[number]]
        right = rights[at_right : at_right + steps[number][0]]
        at_left += counts[number]
        at_right += steps[number][0]

        @pl.when(step == start)
        def _():
            turned[...] = jnp.concatenate(assemble(left), axis=0).T

        @pl.when((step >= start) & (step < start + steps[number][1]))
        def _():
            b = jnp.concatenate([r[0] if len(r.shape) == 3 else r[...] for r in right], axis=0)
            total[...] = dot(turned[...], b).astype(BF16)

        start += steps[number][1]
    for d in range(4):
        for place, offset in enumerate(rows_of(first, d, place_ref)):
            outs[d][place * 48 : (place + 1) * 48, :] = total[pl.ds(offset, 48), :]


def grads(first, place, terms):
    lefts, specs, rights, right_specs = [], [], [], []
    counts, steps, start = [], [], 0
    for left, right, number in terms:
        lefts += left
        specs += [whole(a.shape) for a in left]
        counts.append(len(left))
        steps.append((len(right), number))
        for array, block, index in right:
            rights.append(array)
            right_specs.append(
                pl.BlockSpec(
                    block,
                    lambda j, s=start, n=number, index=index: index(jnp.clip(j - s, 0, n - 1)),
                )
            )
        start += number
    out = pl.BlockSpec((384, NB), lambda j: (0, j))
    columns = start * NB
    return pl.pallas_call(
        functools.partial(grad_kernel, first, counts, steps),
        out_shape=(jax.ShapeDtypeStruct((384, columns), BF16),) * 4,
        in_specs=[SMEM] + specs + right_specs,
        out_specs=(out,) * 4,
        scratch_shapes=[pltpu.VMEM((D, 2 * HALF), BF16), pltpu.VMEM((D, NB), BF16)],
        grid=(start,),
        compiler_params=params(40),
        cost_estimate=cost(2 * 2 * HALF * D * columns, 2 * D * columns + 2 * 2 * HALF * (columns + D)),
        name="grads",
    )(place, *lefts, *rights)


def sum_kernel(first, place_ref, a_ref, b_ref, c_ref, d_ref, o0, o1, o2, o3, total):
    t = a_ref[...].astype(F32) + b_ref[...].astype(F32) + c_ref[...].astype(F32) + d_ref[...].astype(F32)
    total[...] = t.astype(BF16)
    here = place_ref[1 if first else 0]
    for d, out in enumerate((o0, o1, o2, o3)):
        at = lax.rem(here + d, 4)
        for major in range(2):
            offset = pl.multiple_of((major * 4 + at) * 48, 16)
            out[major * 48 : (major + 1) * 48, :] = total[pl.ds(offset, 48), :]


def sum_ring(first, place, parts):
    columns = parts[0].shape[1]
    spec = pl.BlockSpec((384, NB), lambda j: (0, j))
    out = pl.BlockSpec((96, NB), lambda j: (0, j))
    return pl.pallas_call(
        functools.partial(sum_kernel, first),
        out_shape=(jax.ShapeDtypeStruct((96, columns), BF16),) * 4,
        in_specs=[SMEM] + [spec] * 4,
        out_specs=(out,) * 4,
        scratch_shapes=[pltpu.VMEM((384, NB), BF16)],
        grid=(columns // NB,),
        compiler_params=params(16),
        cost_estimate=cost(4 * 384 * columns, 10 * 384 * columns),
        name="sum_ring",
    )(place, *parts)


def last_kernel(place_ref, *refs):
    ins, (keep, away, total) = refs[:-3], refs[-3:]
    half = len(ins) // 2
    here = place_ref[2]
    columns = ins[0].shape[1]
    for number in range(2):
        t = sum(r[...].astype(F32) for r in ins[number * half : (number + 1) * half])
        total[:, number * columns : (number + 1) * columns] = t
    keep[...] = total[pl.ds(pl.multiple_of(here * 48, 16), 48), :]
    away[...] = total[pl.ds(pl.multiple_of((1 - here) * 48, 16), 48), :].astype(BF16)


def sum_last(place, parts_x, parts_y):
    columns = parts_x[0].shape[1]
    return pl.pallas_call(
        last_kernel,
        out_shape=(
            jax.ShapeDtypeStruct((48, 2 * columns), F32),
            jax.ShapeDtypeStruct((48, 2 * columns), BF16),
        ),
        in_specs=[SMEM] + [whole((96, columns))] * 8,
        out_specs=(whole((48, 2 * columns)),) * 2,
        scratch_shapes=[pltpu.VMEM((96, 2 * columns), F32)],
        grid=(1,),
        compiler_params=params(24),
        cost_estimate=cost(8 * 96 * columns, 24 * 96 * columns),
        name="sum_last",
    )(place, *parts_x, *parts_y)


def reduce_pair(place, parts_x, parts_y):
    got_x = [parts_x[0]] + [send(parts_x[d], x_by(d)) for d in (1, 2, 3)]
    got_y = [parts_y[0]] + [send(parts_y[d], y_by(d)) for d in (1, 2, 3)]
    next_x = sum_ring(True, place, got_x)
    next_y = sum_ring(False, place, got_y)
    got_x = [next_x[0]] + [send(next_x[d], y_by(d)) for d in (1, 2, 3)]
    got_y = [next_y[0]] + [send(next_y[d], x_by(d)) for d in (1, 2, 3)]
    keep, away = sum_last(place, got_x, got_y)
    return keep + send(away, ZLO).astype(F32)


def body(tokens, norm_gain, norm_shift, w_qkv, w_out, w_up, w_down, granularity, cotangent):
    zl, y, x, zh, c = (lax.axis_index(a) for a in AXES)
    layers = w_qkv.shape[0]
    core = c.reshape(1).astype(jnp.int32)
    place = jnp.stack([x, y, zl]).astype(jnp.int32)
    width = FF // 8 * 2 ** granularity[0, 0] - (zh * 2 + c) * SLICE
    width = width.reshape(1).astype(jnp.int32)
    w_qkv = jnp.transpose(w_qkv, (0, 2, 1, 3))
    low_chip = zh == 0

    positions = (jnp.arange(2 * HALF, dtype=jnp.int32) ^ (c * OWN)).astype(F32)[:, None]
    half = E // 2
    frequency = BASE ** (-jnp.arange(half, dtype=F32) / half)
    angles = positions * frequency[None, :]
    cos = jnp.cos(angles)
    sin = jnp.sin(angles)
    cos = jnp.concatenate([cos, cos], axis=1)
    sin = jnp.concatenate([-sin, sin], axis=1)

    def gain(layer, member):
        return norm_gain[layer, member][None, :]

    def shift(layer, member):
        return norm_shift[layer, member][None, :]

    def both_chunks(own):
        other = send(own, FAR)
        return jnp.where(low_chip, own, other), jnp.where(low_chip, other, own)

    def exchange(mine, theirs):
        s = mine.astype(F32) + send(theirs, CORE).astype(F32)
        s = s.astype(BF16)
        return s, send(s, FAR)

    whole_piece = whole((OWN, D))

    def swap(a):
        return (a, whole_piece), (send(a, CORE), whole_piece)

    stream = list(both_chunks(tokens))
    normed = [swap(norm(stream[k], gain(0, 0), shift(0, 0))) for k in range(2)]
    saved = []
    last = None
    for layer in range(layers):
        keep = {"stream": list(stream), "normed": normed}
        qkv, mixture, sums = [None] * 2, [None] * 2, [None] * 2
        mid, normed_two = [None] * 2, [None] * 2
        hid, slope = [None] * 2, [None] * 2
        for k in range(2):
            qkv[k], mixture[k], pm, pt = attend(
                layer, k, core, *normed[k], w_qkv, w_out, cos, sin, qkv[0]
            )
            sums[k] = exchange(pm, pt)
        for k in range(2):
            mid[k], a = add_norm(stream[k], *sums[k], gain(layer, 1), shift(layer, 1))
            normed_two[k] = swap(a)
        following = [None] * 2
        parts = [None] * 2
        for k in range(2):
            am, at = normed_two[k]
            hid[k], slope[k], pm, pt = feed(layer, width, am[0], at[0], w_up, w_down)
            if layer < layers - 1:
                sums[k] = exchange(pm, pt)
            else:
                parts[k] = (pm, pt)
        keep.update(qkv=qkv, mixture=mixture, mid=mid, normed_two=normed_two, hid=hid, slope=slope)
        saved.append(keep)
        if layer < layers - 1:
            for k in range(2):
                stream[k], a = add_norm(mid[k], *sums[k], gain(layer + 1, 0), shift(layer + 1, 0))
                following[k] = swap(a)
            normed = following
        else:
            s = [
                parts[k][0].astype(F32) + send(parts[k][1], CORE).astype(F32) for k in range(2)
            ]
            ours = jnp.where(low_chip, s[0], s[1])
            away = jnp.where(low_chip, s[1], s[0]).astype(BF16)
            base = jnp.where(low_chip, mid[0], mid[1])
            last = (base + (ours + send(away, FAR).astype(F32))).astype(BF16)

    gradient = jnp.concatenate(both_chunks(cotangent), axis=0)
    gm = gradient
    gt = send(gm, CORE)
    weight_grads = [None] * layers
    norm_sums = [[None, None] for _ in range(layers)]
    for layer in reversed(range(layers)):
        kept = saved[layer]
        a_two = [p[0] for k in range(2) for p in kept["normed_two"][k]]
        a_one = [p[0] for k in range(2) for p in kept["normed"][k]]
        du, pm, pt = feed_back(layer, gm, gt, w_up, w_down, *kept["slope"])
        s, r = exchange(pm, pt)

        def column(j):
            return (0, j)

        up_parts = grads(True, place, [(a_two, [(du, (2 * HALF, NB), column)], SLICE // NB)])
        down_parts = grads(
            False, place, [([gm, gt], [(h, (HALF, NB), column) for h in kept["hid"]], SLICE // NB)]
        )
        feed_grad = reduce_pair(place, up_parts, down_parts)
        gradient, gm, norm_sums[layer][1] = norm_back(*kept["mid"], s, r, gradient, gain(layer, 1))
        gt = send(gm, CORE)
        dqkv, pm, pt = attend_back(layer, core, gm, gt, w_qkv, w_out, cos, sin, *kept["qkv"])
        s, r = exchange(pm, pt)
        first = grads(
            True, place, [(a_one, [(dqkv, (1, 2 * HALF, NB), lambda j: (j, 0, 0))], 2)]
        )
        second = grads(
            False,
            place,
            [
                (a_one, [(dqkv, (1, 2 * HALF, NB), lambda j: (2, 0, 0))], 1),
                ([gm, gt], [(m, (HALF, NB), lambda j: (0, 0)) for m in kept["mixture"]], 1),
            ],
        )
        attend_grad = reduce_pair(place, first, second)
        gradient, gm, norm_sums[layer][0] = norm_back(
            *kept["stream"], s, r, gradient, gain(layer, 0)
        )
        if layer:
            gt = send(gm, CORE)
        weight_grads[layer] = (feed_grad, attend_grad)

    input_grad = jnp.where(low_chip, gradient[:OWN], gradient[OWN:])
    sums = jnp.stack([norm_sums[layer][member] for layer in range(layers) for member in range(2)])
    for perm in (CORE, x_flip(1), x_flip(2), y_flip(1), y_flip(2), ZLO):
        sums = sums + send(sums, perm)
    sums = sums.reshape(layers, 2, 2, D)
    gain_grads, shift_grads = sums[:, :, 0], sums[:, :, 1]

    feed_grads = jnp.stack([w[0] for w in weight_grads])
    attend_grads = jnp.stack([w[1] for w in weight_grads])
    grad_up = feed_grads[:, :, :SLICE]
    grad_down = jnp.swapaxes(feed_grads[:, :, SLICE:], 1, 2)
    grad_qkv = attend_grads[:, :, : 3 * HID].reshape(layers, 48, 3, HID)
    grad_out = jnp.swapaxes(attend_grads[:, :, 3 * HID :], 1, 2)
    return (
        last,
        input_grad,
        grad_qkv,
        grad_out,
        grad_up,
        grad_down,
        gain_grads,
        shift_grads,
        shift_grads[:, 1, :],
    )


def solution(mesh):
    fine = Mesh(mesh.devices.reshape(SIZES), AXES)
    rows = P(AXES, None)
    dp, tensor = AXES[:3], AXES[3:]
    return jax.shard_map(
        body,
        mesh=fine,
        in_specs=(
            rows,
            P(),
            P(),
            P(None, None, None, tensor),
            P(None, tensor, None),
            P(None, None, tensor),
            P(None, tensor, None),
            P(dp, None),
            rows,
        ),
        out_specs=(
            rows,
            rows,
            P(None, dp, None, tensor),
            P(None, tensor, dp),
            P(None, dp, tensor),
            P(None, tensor, dp),
            P(),
            P(),
            P(),
        ),
        check_vma=False,
    )
```

```python
import functools
import itertools

import jax
import jax.numpy as jnp
from jax import lax
from jax.experimental import pallas as pl
from jax.experimental.pallas import tpu as pltpu
from jax.sharding import Mesh
from jax.sharding import PartitionSpec as P

D = 1536
FF = 6144
E = 128
HEADS = 3
HID = HEADS * E
SLICE = 1536
HALF = 256
OWN = 128
FB = 512
EPS = 1e-5
BASE = 10000.0
MASKED = -1e30
SCALE = E**-0.5
C1 = 0.7978845608028654
C2 = 0.044715

AXES = ("zl", "y", "x", "zh", "c")
SIZES = (2, 4, 4, 2, 2)
F32 = jnp.float32
BF16 = jnp.bfloat16


def flat(place):
    index = 0
    for size, at in zip(SIZES, place):
        index = index * size + at
    return index


def pairs(move):
    return [
        (flat(p), flat(move(*p))) for p in itertools.product(*[range(s) for s in SIZES])
    ]


CORE = pairs(lambda zl, y, x, zh, c: (zl, y, x, zh, 1 - c))
FAR = pairs(lambda zl, y, x, zh, c: (zl, y, x, 1 - zh, c))
ZLO = pairs(lambda zl, y, x, zh, c: (1 - zl, y, x, zh, c))


def x_by(d):
    return pairs(lambda zl, y, x, zh, c: (zl, y, (x + d) % 4, zh, c))


def y_by(d):
    return pairs(lambda zl, y, x, zh, c: (zl, (y + d) % 4, x, zh, c))


def x_flip(d):
    return pairs(lambda zl, y, x, zh, c: (zl, y, x ^ d, zh, c))


def y_flip(d):
    return pairs(lambda zl, y, x, zh, c: (zl, y ^ d, x, zh, c))


def send(values, perm):
    return lax.ppermute(values, AXES, perm)


def dot(a, b):
    return jnp.dot(a, b, preferred_element_type=F32)


def dot_t(a, b):
    return lax.dot_general(a, b, (((1,), (1,)), ((), ())), preferred_element_type=F32)


def t_dot(a, b):
    return lax.dot_general(a, b, (((0,), (0,)), ((), ())), preferred_element_type=F32)


VMEM_MB = {'attend':16,'attend_back':26,'feed':18,'feed_back':26,'grads':32,'merge':16,'sum_rings':16,'sum_last':16,'norm':8,'add_norm':8,'norm_back':24}


def params(mb):
    return pltpu.CompilerParams(vmem_limit_bytes=mb * 1024 * 1024)


def cost(flops, size, trans=0):
    return pl.CostEstimate(flops=1, bytes_accessed=1, transcendentals=0)


def whole(shape):
    zeros = (0,) * len(shape)
    return pl.BlockSpec(shape, lambda *_: zeros)


SMEM = pl.BlockSpec(memory_space=pltpu.SMEM)
ANY = pl.BlockSpec(memory_space=pl.ANY)


def run(kernel, args, in_specs, out_shape, out_specs, grid, name, estimate, scratch=(), after=()):
    count, extra = len(args), len(after)

    def wrapped(*refs):
        kernel(*refs[:count], *refs[count + extra :])

    return pl.pallas_call(
        wrapped,
        out_shape=out_shape,
        in_specs=list(in_specs) + [ANY] * extra,
        out_specs=out_specs,
        scratch_shapes=list(scratch),
        grid=(grid,),
        compiler_params=params(VMEM_MB[name]),
        cost_estimate=estimate,
        name=name,
    )(*args, *after)


def moments(x):
    mean = jnp.mean(x, axis=-1, keepdims=True)
    centered = x - mean
    var = jnp.mean(centered * centered, axis=-1, keepdims=True)
    return centered, lax.rsqrt(var + EPS)


def norm_kernel(x_ref, g_ref, b_ref, a_ref):
    centered, r = moments(x_ref[...].astype(F32))
    a_ref[...] = (centered * r * g_ref[...] + b_ref[...]).astype(BF16)


def norm(x, gain, shift):
    rows = x.shape[0]
    return run(
        norm_kernel,
        (x, gain, shift),
        [whole((rows, D)), whole((1, D)), whole((1, D))],
        jax.ShapeDtypeStruct((rows, D), BF16),
        whole((rows, D)),
        1,
        "norm",
        cost(10 * rows * D, 6 * rows * D),
    )


def add_norm_kernel(x_ref, s_ref, r_ref, g_ref, b_ref, m_ref, a_ref):
    x = x_ref[...].astype(F32) + (s_ref[...].astype(F32) + r_ref[...].astype(F32))
    m_ref[...] = x
    centered, r = moments(x)
    a_ref[...] = (centered * r * g_ref[...] + b_ref[...]).astype(BF16)


def add_norm(x, s, r, gain, shift, after=()):
    rows = x.shape[0]
    return run(
        add_norm_kernel,
        (x, s, r, gain, shift),
        [whole((rows, D))] * 3 + [whole((1, D))] * 2,
        (jax.ShapeDtypeStruct((rows, D), F32), jax.ShapeDtypeStruct((rows, D), BF16)),
        (whole((rows, D)), whole((rows, D))),
        1,
        "add_norm",
        cost(10 * rows * D, 14 * rows * D),
        after=after,
    )


def norm_back_kernel(count, *refs):
    xs, ss, rs, prevs = (refs[n * count : (n + 1) * count] for n in range(4))
    g_ref, refs = refs[4 * count], refs[4 * count + 1 :]
    ds, lows, sums_ref = refs[:count], refs[count : 2 * count], refs[2 * count]
    for k in range(count):
        da = ss[k][...].astype(F32) + rs[k][...].astype(F32)
        centered, r = moments(xs[k][...].astype(F32))
        xh = centered * r
        e = da * g_ref[...]
        mean_e = jnp.mean(e, axis=-1, keepdims=True)
        mean_ex = jnp.mean(e * xh, axis=-1, keepdims=True)
        out = prevs[k][...].astype(F32) + r * (e - mean_e - xh * mean_ex)
        ds[k][...] = out
        lows[k][...] = out.astype(BF16)
        both = (jnp.sum(da * xh, axis=0, keepdims=True), jnp.sum(da, axis=0, keepdims=True))
        for n in range(2):
            if k:
                sums_ref[n : n + 1, :] += both[n]
            else:
                sums_ref[n : n + 1, :] = both[n]


def norm_back(xs, ss, rs, prevs, gain, after=()):
    count = len(xs)
    piece = whole((OWN, D))
    outs = run(
        functools.partial(norm_back_kernel, count),
        (*xs, *ss, *rs, *prevs, gain),
        [piece] * (4 * count) + [whole((1, D))],
        (jax.ShapeDtypeStruct((OWN, D), F32),) * count
        + (jax.ShapeDtypeStruct((OWN, D), BF16),) * count
        + (jax.ShapeDtypeStruct((2, D), F32),),
        (piece,) * (2 * count) + (whole((2, D)),),
        1,
        "norm_back",
        cost(20 * count * OWN * D, 18 * count * OWN * D),
        after=after,
    )
    return outs[:count], outs[count : 2 * count], outs[2 * count]


def rot(x, cos, sin):
    return x * cos + pltpu.roll(x, E // 2, 1) * sin


def allowed(q_start, rows, columns):
    q = lax.broadcasted_iota(jnp.int32, (rows, columns), 0) + q_start
    return lax.broadcasted_iota(jnp.int32, (rows, columns), 1) <= q


def mine_theirs(core, acc, chunks, outs):
    for k in range(chunks):
        for out, side in zip(outs[2 * k : 2 * k + 2], (core, 1 - core)):
            rows = pl.ds(pl.multiple_of(k * HALF + side * OWN, OWN), OWN)
            out[...] = acc[rows, :].astype(BF16)


def softmax(s):
    top = jnp.max(s, axis=-1, keepdims=True)
    e = jnp.exp(s - top)
    return e / jnp.sum(e, axis=-1, keepdims=True)


def attend_kernel(chunk, core_ref, a_ref, w_ref, wo_ref, cos_ref, sin_ref, *rest):
    if chunk:
        before_ref, qkv_ref, o_ref, pm_ref, pt_ref, acc = rest
    else:
        qkv_ref, o_ref, pm_ref, pt_ref, acc = rest
    step = pl.program_id(0)
    a = a_ref[...]
    w = jnp.concatenate([w_ref[0, 0], w_ref[0, 1], w_ref[0, 2]], axis=1)
    p = dot(a, w)
    cos, sin = cos_ref[...], sin_ref[...]
    q = (rot(p[:, :E], cos, sin) * SCALE).astype(BF16)
    k = rot(p[:, E : 2 * E], cos, sin).astype(BF16)
    v = p[:, 2 * E :].astype(BF16)
    qkv_ref[0], qkv_ref[1], qkv_ref[2] = q, k, v
    if chunk:
        k = jnp.concatenate([before_ref[1], k], axis=0)
        v = jnp.concatenate([before_ref[2], v], axis=0)
    s = dot_t(q, k)
    s = jnp.where(allowed(chunk * HALF, HALF, s.shape[1]), s, MASKED)
    o = dot(softmax(s).astype(BF16), v).astype(BF16)
    o_ref[...] = o
    part = dot(o, wo_ref[0])

    @pl.when(step == 0)
    def _():
        acc[...] = part

    @pl.when(step > 0)
    def _():
        acc[...] += part

    @pl.when(step == HEADS - 1)
    def _():
        mine_theirs(core_ref[0], acc, 1, (pm_ref, pt_ref))


def attend(layer, chunk, core, a, w_qkv, w_out, cos, sin, before, after=()):
    head = pl.BlockSpec((3, HALF, E), lambda h: (0, 0, h))
    tables = pl.BlockSpec((HALF, E), lambda h: (chunk, 0))
    piece = whole((OWN, D))
    return run(
        functools.partial(attend_kernel, chunk),
        (core, a, w_qkv, w_out, cos, sin) + ((before,) if chunk else ()),
        [
            SMEM,
            whole((HALF, D)),
            pl.BlockSpec((1, 3, D, E), lambda h: (layer, 0, 0, h)),
            pl.BlockSpec((1, E, D), lambda h: (layer, h, 0)),
            tables,
            tables,
        ]
        + ([head] if chunk else []),
        (
            jax.ShapeDtypeStruct((3, HALF, HID), BF16),
            jax.ShapeDtypeStruct((HALF, HID), BF16),
            jax.ShapeDtypeStruct((OWN, D), BF16),
            jax.ShapeDtypeStruct((OWN, D), BF16),
        ),
        (head, pl.BlockSpec((HALF, E), lambda h: (0, h)), piece, piece),
        HEADS,
        "attend",
        cost(2 * HALF * D * 4 * HID, 2 * 4 * HID * D + 8 * HALF * D),
        scratch=[pltpu.VMEM((HALF, D), F32)],
        after=after,
    )


def attend_back_kernel(
    core_ref, g0_ref, g1_ref, w_ref, wo_ref, cos_ref, sin_ref, c0_ref, c1_ref, d_ref, *rest
):
    outs, acc = rest[:4], rest[4]
    step = pl.program_id(0)
    do0 = dot_t(g0_ref[...], wo_ref[0]).astype(BF16)
    do1 = dot_t(g1_ref[...], wo_ref[0]).astype(BF16)
    k = jnp.concatenate([c0_ref[1], c1_ref[1]], axis=0)
    v = jnp.concatenate([c0_ref[2], c1_ref[2]], axis=0)

    def block(chunk, q, do, keys, values):
        s = dot_t(q, keys)
        s = jnp.where(allowed(chunk * HALF, HALF, s.shape[1]), s, MASKED)
        prob = softmax(s)
        dp = dot_t(do, values)
        ds = (prob * (dp - jnp.sum(prob * dp, axis=-1, keepdims=True))).astype(BF16)
        return dot(ds, keys), t_dot(ds, q), t_dot(prob.astype(BF16), do)

    dq1, dk1, dv1 = block(1, c1_ref[0], do1, k, v)
    dq0, dk0, dv0 = block(0, c0_ref[0], do0, c0_ref[1], c0_ref[2])
    cos, sin = cos_ref[...], -sin_ref[...]
    dq = (rot(jnp.concatenate([dq0, dq1], axis=0), cos, sin) * SCALE).astype(BF16)
    dk = jnp.concatenate([dk0 + dk1[:HALF], dk1[HALF:]], axis=0)
    dk = rot(dk, cos, sin).astype(BF16)
    dv = jnp.concatenate([dv0 + dv1[:HALF], dv1[HALF:]], axis=0).astype(BF16)
    d_ref[0], d_ref[1], d_ref[2] = dq, dk, dv
    w = jnp.concatenate([w_ref[0, 0], w_ref[0, 1], w_ref[0, 2]], axis=1)
    part = dot_t(jnp.concatenate([dq, dk, dv], axis=1), w)

    @pl.when(step == 0)
    def _():
        acc[...] = part

    @pl.when(step > 0)
    def _():
        acc[...] += part

    @pl.when(step == HEADS - 1)
    def _():
        mine_theirs(core_ref[0], acc, 2, outs)


def attend_back(layer, core, g0, g1, w_qkv, w_out, cos, sin, saved0, saved1, after=()):
    rows = 2 * HALF
    head = pl.BlockSpec((3, HALF, E), lambda h: (0, 0, h))
    piece = whole((HALF, D))
    return run(
        attend_back_kernel,
        (core, g0, g1, w_qkv, w_out, cos, sin, saved0, saved1),
        [
            SMEM,
            piece,
            piece,
            pl.BlockSpec((1, 3, D, E), lambda h: (layer, 0, 0, h)),
            pl.BlockSpec((1, E, D), lambda h: (layer, h, 0)),
            whole((rows, E)),
            whole((rows, E)),
            head,
            head,
        ],
        (
            jax.ShapeDtypeStruct((3, rows, HID), BF16),
        )
        + (jax.ShapeDtypeStruct((OWN, D), BF16),) * 4,
        (pl.BlockSpec((3, rows, E), lambda h: (0, 0, h)),) + (whole((OWN, D)),) * 4,
        HEADS,
        "attend_back",
        cost(2 * rows * D * 5 * HID, 2 * 4 * HID * D + 8 * rows * D),
        scratch=[pltpu.VMEM((rows, D), F32)],
        after=after,
    )


def feed_kernel(width_ref, core_ref, a_ref, up_ref, down_ref, hid_ref, slope_ref, pm_ref, pt_ref, acc):
    step = pl.program_id(0)
    u = dot(a_ref[...], up_ref[0])
    place = lax.broadcasted_iota(jnp.int32, u.shape, 1) + step * FB
    keep = place < width_ref[0]
    square = u * u
    t = jnp.tanh(C1 * (u + C2 * u * square))
    hid = jnp.where(keep, 0.5 * u * (1.0 + t), 0.0).astype(BF16)
    slope = 0.5 * (1.0 + t) + 0.5 * u * (1.0 - t * t) * (C1 * (1.0 + 3.0 * C2 * square))
    slope_ref[...] = jnp.where(keep, slope, 0.0).astype(BF16)
    hid_ref[...] = hid
    part = dot(hid, down_ref[0])

    @pl.when(step == 0)
    def _():
        acc[...] = part

    @pl.when(step > 0)
    def _():
        acc[...] += part

    @pl.when(step == SLICE // FB - 1)
    def _():
        mine_theirs(core_ref[0], acc, 1, (pm_ref, pt_ref))


def feed(layer, width, core, a, w_up, w_down, after=()):
    piece = whole((OWN, D))
    block = pl.BlockSpec((HALF, FB), lambda j: (0, j))
    return run(
        feed_kernel,
        (width, core, a, w_up, w_down),
        [
            SMEM,
            SMEM,
            whole((HALF, D)),
            pl.BlockSpec((1, D, FB), lambda j: (layer, 0, j)),
            pl.BlockSpec((1, FB, D), lambda j: (layer, j, 0)),
        ],
        (
            jax.ShapeDtypeStruct((HALF, SLICE), BF16),
            jax.ShapeDtypeStruct((HALF, SLICE), BF16),
            jax.ShapeDtypeStruct((OWN, D), BF16),
            jax.ShapeDtypeStruct((OWN, D), BF16),
        ),
        (block, block, piece, piece),
        SLICE // FB,
        "feed",
        cost(4 * HALF * D * SLICE, 4 * SLICE * D + 8 * HALF * D),
        scratch=[pltpu.VMEM((HALF, D), F32)],
        after=after,
    )


def feed_back_kernel(core_ref, g0_ref, g1_ref, down_ref, up_ref, slope0_ref, slope1_ref, du_ref, *rest):
    outs, acc = rest[:4], rest[4]
    step = pl.program_id(0)
    g = jnp.concatenate([g0_ref[...], g1_ref[...]], axis=0)
    dhid = dot_t(g, down_ref[0])
    slope = jnp.concatenate([slope0_ref[...], slope1_ref[...]], axis=0).astype(F32)
    du = (dhid * slope).astype(BF16)
    du_ref[...] = du
    part = dot_t(du, up_ref[0])

    @pl.when(step == 0)
    def _():
        acc[...] = part

    @pl.when(step > 0)
    def _():
        acc[...] += part

    @pl.when(step == SLICE // FB - 1)
    def _():
        mine_theirs(core_ref[0], acc, 2, outs)


def feed_back(layer, core, g0, g1, w_up, w_down, slope0, slope1, after=()):
    rows = 2 * HALF
    piece = whole((HALF, D))
    block = pl.BlockSpec((HALF, FB), lambda j: (0, j))
    return run(
        feed_back_kernel,
        (core, g0, g1, w_down, w_up, slope0, slope1),
        [
            SMEM,
            piece,
            piece,
            pl.BlockSpec((1, FB, D), lambda j: (layer, j, 0)),
            pl.BlockSpec((1, D, FB), lambda j: (layer, 0, j)),
            block,
            block,
        ],
        (
            jax.ShapeDtypeStruct((rows, SLICE), BF16),
        )
        + (jax.ShapeDtypeStruct((OWN, D), BF16),) * 4,
        (pl.BlockSpec((rows, FB), lambda j: (0, j)),) + (whole((OWN, D)),) * 4,
        SLICE // FB,
        "feed_back",
        cost(4 * rows * D * SLICE, 4 * SLICE * D + 8 * rows * D),
        scratch=[pltpu.VMEM((rows, D), F32)],
        after=after,
    )


def grad_kernel(first, counts, steps, place_ref, *refs):
    lefts, refs = refs[: sum(counts)], refs[sum(counts) :]
    rights, refs = refs[: sum(n for n, _ in steps)], refs[sum(n for n, _ in steps) :]
    own, to_right, to_left, right_later, left_later, turned, total = refs
    step = pl.program_id(0)
    start = at_left = at_right = 0
    for count, (operands, number) in zip(counts, steps):
        left = lefts[at_left : at_left + count]
        right = rights[at_right : at_right + operands]
        at_left += count
        at_right += operands

        @pl.when(step == start)
        def _():
            turned[...] = jnp.concatenate([r[...] for r in left], axis=0).T

        @pl.when((step >= start) & (step < start + number))
        def _():
            b = jnp.concatenate([r[0] if len(r.shape) == 3 else r[...] for r in right], axis=0)
            total[...] = dot(turned[...], b).astype(BF16)

        start += number

    def put(out, at, d, major):
        there = lax.rem(place_ref[0 if first else 1] + d, 4)
        for minor in range(4):
            block = (major * 4 + minor) * 4 + there if first else (major * 4 + there) * 4 + minor
            out[(at + minor) * 48 : (at + minor + 1) * 48, :] = total[
                pl.ds(pl.multiple_of(block * 48, 16), 48), :
            ]

    put(own, 0, 0, 0)
    put(own, 4, 0, 1)
    put(to_right, 0, 2, 1)
    put(to_right, 4, 1, 0)
    put(to_left, 0, 2, 0)
    put(to_left, 4, 3, 1)
    put(right_later, 0, 1, 1)
    put(left_later, 0, 3, 0)


def grads(first, place, block, terms, after=()):
    lefts, specs, rights, right_specs = [], [], [], []
    counts, steps, start = [], [], 0
    for left, right, number in terms:
        lefts += left
        specs += [whole(a.shape) for a in left]
        counts.append(len(left))
        steps.append((len(right), number))
        for array, shape, index in right:
            rights.append(array)
            right_specs.append(
                pl.BlockSpec(
                    shape,
                    lambda j, s=start, n=number, index=index: index(jnp.clip(j - s, 0, n - 1)),
                )
            )
        start += number
    columns = start * block
    rows = (384, 384, 384, 192, 192)
    return run(
        functools.partial(grad_kernel, first, counts, steps),
        (place, *lefts, *rights),
        [SMEM] + specs + right_specs,
        tuple(jax.ShapeDtypeStruct((n, columns), BF16) for n in rows),
        tuple(pl.BlockSpec((n, block), lambda j: (0, j)) for n in rows),
        start,
        "grads",
        cost(4 * HALF * D * columns, 3 * D * columns + 4 * HALF * (columns + D)),
        scratch=[pltpu.VMEM((D, 2 * HALF), BF16), pltpu.VMEM((D, block), BF16)],
        after=after,
    )


def merge_kernel(*refs):
    ins, outs = refs[:8], refs[8:]
    for number, out in enumerate(outs):
        own, got = ins[2 * number : 2 * number + 2]
        out[...] = (own[...].astype(F32) + got[...].astype(F32)).astype(BF16)


def merge(pieces, after=()):
    columns = pieces[0][0].shape[1]
    block = min(columns, 768)
    spec = pl.BlockSpec((192, block), lambda j: (0, j))
    return run(
        merge_kernel,
        [array for pair in pieces for array in pair],
        [spec] * 8,
        (jax.ShapeDtypeStruct((192, columns), BF16),) * 4,
        (spec,) * 4,
        columns // block,
        "merge",
        cost(4 * 192 * columns, 24 * 192 * columns),
        after=after,
    )


def sum_kernel(place_ref, *refs):
    ins, outs, total = refs[:10], refs[10:18], refs[18]
    for number, first in enumerate((True, False)):
        own, left_a, right_b, right_a, left_b = ins[5 * number : 5 * number + 5]
        for at, one, two in ((0, left_a, right_a), (192, right_b, left_b)):
            t = own[at : at + 192].astype(F32) + one[...].astype(F32) + two[...].astype(F32)
            total[at : at + 192] = t.astype(BF16)
        here = place_ref[1 if first else 0]
        for d in range(4):
            there = lax.rem(here + d, 4)
            for major in range(2):
                offset = pl.multiple_of((major * 4 + there) * 48, 16)
                outs[4 * number + d][major * 48 : (major + 1) * 48, :] = total[pl.ds(offset, 48), :]


def sum_rings(place, rings, after=()):
    columns = rings[0][0].shape[1]
    block = 384
    upper = pl.BlockSpec((192, block), lambda j: (0, j))
    lower = pl.BlockSpec((192, block), lambda j: (1, j))
    full = pl.BlockSpec((384, block), lambda j: (0, j))
    outs = run(
        sum_kernel,
        [place] + [array for ring in rings for array in ring],
        [SMEM] + [full, lower, lower, upper, upper] * 2,
        (jax.ShapeDtypeStruct((96, columns), BF16),) * 8,
        (pl.BlockSpec((96, block), lambda j: (0, j)),) * 8,
        columns // block,
        "sum_rings",
        cost(6 * 384 * columns, 16 * 384 * columns),
        scratch=[pltpu.VMEM((384, block), BF16)],
        after=after,
    )
    return outs[:4], outs[4:]


def last_kernel(place_ref, *refs):
    ins, (keep, away, total) = refs[:-3], refs[-3:]
    half = len(ins) // 2
    here = place_ref[2]
    columns = ins[0].shape[1]
    for number in range(2):
        t = sum(r[...].astype(F32) for r in ins[number * half : (number + 1) * half])
        total[:, number * columns : (number + 1) * columns] = t
    keep[...] = total[pl.ds(pl.multiple_of(here * 48, 16), 48), :]
    away[...] = total[pl.ds(pl.multiple_of((1 - here) * 48, 16), 48), :].astype(BF16)


def sum_last(place, parts_x, parts_y, after=()):
    columns = parts_x[0].shape[1]
    return run(
        last_kernel,
        (place, *parts_x, *parts_y),
        [SMEM] + [whole((96, columns))] * 8,
        (
            jax.ShapeDtypeStruct((48, 2 * columns), F32),
            jax.ShapeDtypeStruct((48, 2 * columns), BF16),
        ),
        (whole((48, 2 * columns)),) * 2,
        1,
        "sum_last",
        cost(8 * 96 * columns, 24 * 96 * columns),
        scratch=[pltpu.VMEM((96, 2 * columns), F32)],
        after=after,
    )


class Reduction:
    def __init__(self, place, parts_x, parts_y):
        self.place = place
        self.own = parts_x[0], parts_y[0]
        self.later = parts_x[3:], parts_y[3:]
        self.rings = (x_by(1), x_by(3)), (y_by(1), y_by(3))
        self.from_left = [send(p[1], r[0]) for p, r in zip((parts_x, parts_y), self.rings)]
        self.from_right = [send(p[2], r[1]) for p, r in zip((parts_x, parts_y), self.rings)]

    def merge(self, after=()):
        pieces = []
        for n in range(2):
            pieces += [(self.later[n][0], self.from_left[n]), (self.later[n][1], self.from_right[n])]
        outs = merge(pieces, after)
        self.left_b = [send(outs[2 * n], self.rings[n][0]) for n in range(2)]
        self.right_a = [send(outs[2 * n + 1], self.rings[n][1]) for n in range(2)]
        return outs

    def sum(self, after=()):
        rings = [
            (self.own[n], self.from_left[n], self.from_right[n], self.right_a[n], self.left_b[n])
            for n in range(2)
        ]
        next_x, next_y = outs = sum_rings(self.place, rings, after)
        self.got_x = [next_x[0]] + [send(next_x[d], y_by(d)) for d in (1, 2, 3)]
        self.got_y = [next_y[0]] + [send(next_y[d], x_by(d)) for d in (1, 2, 3)]
        return outs[0]

    def last(self, after=()):
        self.keep, away = sum_last(self.place, self.got_x, self.got_y, after)
        self.arrived = send(away, ZLO)
        return (away,)

    def result(self):
        return self.keep + self.arrived.astype(F32)


def body(tokens, norm_gain, norm_shift, w_qkv, w_out, w_up, w_down, granularity, cotangent):
    zl, y, x, zh, c = (lax.axis_index(a) for a in AXES)
    layers = w_qkv.shape[0]
    core = c.reshape(1).astype(jnp.int32)
    place = jnp.stack([x, y, zl]).astype(jnp.int32)
    width = FF // 8 * 2 ** granularity[0, 0] - (zh * 2 + c) * SLICE
    width = width.reshape(1).astype(jnp.int32)
    w_qkv = jnp.transpose(w_qkv, (0, 2, 1, 3))
    low_chip = zh == 0

    positions = jnp.arange(2 * HALF, dtype=F32)[:, None]
    half = E // 2
    frequency = BASE ** (-jnp.arange(half, dtype=F32) / half)
    angles = positions * frequency[None, :]
    cos = jnp.cos(angles)
    sin = jnp.sin(angles)
    cos = jnp.concatenate([cos, cos], axis=1)
    sin = jnp.concatenate([-sin, sin], axis=1)

    def gain(layer, member):
        return norm_gain[layer, member][None, :]

    def shift(layer, member):
        return norm_shift[layer, member][None, :]

    def both_chunks(own):
        other = send(own, FAR)
        return jnp.where(low_chip, own, other), jnp.where(low_chip, other, own)

    def pair(a):
        return lax.all_gather(a, "c", axis=0, tiled=True)

    def core_sum(mine, theirs):
        other = lax.dynamic_slice_in_dim(pair(theirs), (1 - c) * OWN, OWN, 0)
        return mine.astype(F32) + other.astype(F32)

    def exchange(mine, theirs):
        s = core_sum(mine, theirs).astype(BF16)
        return s, send(s, FAR)

    stream = list(both_chunks(tokens))
    normed = [pair(norm(stream[k], gain(0, 0), shift(0, 0))) for k in range(2)]
    saved = []
    gate = ()
    for layer in range(layers):
        keep = {"stream": list(stream), "normed": normed}
        qkv, mixture, sums = [None] * 2, [None] * 2, [None] * 2
        mid, normed_two = [None] * 2, [None] * 2
        hid, slope = [None] * 2, [None] * 2
        for k in range(2):
            qkv[k], mixture[k], pm, pt = attend(
                layer, k, core, normed[k], w_qkv, w_out, cos, sin, qkv[0], gate
            )
            sums[k] = exchange(pm, pt)
            gate = sums[k][:1]
        for k in range(2):
            mid[k], a = add_norm(stream[k], *sums[k], gain(layer, 1), shift(layer, 1), gate)
            normed_two[k] = pair(a)
            hid[k], slope[k], pm, pt = feed(layer, width, core, normed_two[k], w_up, w_down, gate)
            if layer < layers - 1:
                sums[k] = exchange(pm, pt)
                gate = sums[k][:1]
            else:
                sums[k] = core_sum(pm, pt)
        keep.update(qkv=qkv, mixture=mixture, mid=mid, normed_two=normed_two, hid=hid, slope=slope)
        saved.append(keep)
        if layer < layers - 1:
            normed = [None] * 2
            for k in range(2):
                stream[k], a = add_norm(
                    mid[k], *sums[k], gain(layer + 1, 0), shift(layer + 1, 0), gate
                )
                normed[k] = pair(a)
    ours = jnp.where(low_chip, sums[0], sums[1])
    away = jnp.where(low_chip, sums[1], sums[0]).astype(BF16)
    base = jnp.where(low_chip, mid[0], mid[1])
    activations = (base + (ours + send(away, FAR).astype(F32))).astype(BF16)

    gradient = both_chunks(cotangent)
    g = [pair(v) for v in gradient]
    gate = (away,)
    norm_sums = [[None, None] for _ in range(layers)]
    feed_sums, attend_sums = [None] * layers, [None] * layers

    def column(j):
        return (0, j)

    def feed_grads(kept, du, g, after):
        number = SLICE // FB
        up = grads(True, place, FB, [(kept["normed_two"], [(du, (2 * HALF, FB), column)], number)], after)
        down = grads(
            False,
            place,
            FB,
            [(g, [(h, (HALF, FB), column) for h in kept["hid"]], number)],
            (up[4],),
        )
        return Reduction(place, up, down), (down[4],)

    def attend_grads(kept, dqkv, g, after):
        a_one = kept["normed"]
        head = (1, 2 * HALF, HID)
        one = grads(True, place, HID, [(a_one, [(dqkv, head, lambda j: (j, 0, 0))], 2)], after)
        two = grads(
            False,
            place,
            HID,
            [
                (a_one, [(dqkv, head, lambda j: (2, 0, 0))], 1),
                (g, [(m, (HALF, HID), lambda j: (0, 0)) for m in kept["mixture"]], 1),
            ],
            (one[4],),
        )
        return Reduction(place, one, two), (two[4],)

    one, zero = layers - 1, 0
    def backward_sums(parts):
        return list(zip(*[exchange(*parts[2 * k : 2 * k + 2]) for k in range(2)]))

    kept = saved[one]
    du, *parts = feed_back(one, core, *g, w_up, w_down, *kept["slope"], gate)
    ss, rs = backward_sums(parts)
    feed_sums[one], gate = feed_grads(kept, du, g, ss)
    gradient, low, norm_sums[one][1] = norm_back(kept["mid"], ss, rs, gradient, gain(one, 1), gate)
    g = [pair(v) for v in low]
    dqkv, *parts = attend_back(one, core, *g, w_qkv, w_out, cos, sin, *kept["qkv"])
    ss, rs = backward_sums(parts)
    gate = feed_sums[one].merge(ss)[:1]
    attend_sums[one], gate = attend_grads(kept, dqkv, g, gate)
    gradient, low, norm_sums[one][0] = norm_back(
        kept["stream"], ss, rs, gradient, gain(one, 0), gate
    )
    g = [pair(v) for v in low]
    kept = saved[zero]
    du, *parts = feed_back(zero, core, *g, w_up, w_down, *kept["slope"])
    ss, rs = backward_sums(parts)
    gate = feed_sums[one].sum(ss)[:1]
    gate = attend_sums[one].merge(gate)[:1]
    feed_sums[zero], gate = feed_grads(kept, du, g, gate)
    gradient, low, norm_sums[zero][1] = norm_back(
        kept["mid"], ss, rs, gradient, gain(zero, 1), gate
    )
    g = [pair(v) for v in low]
    dqkv, *parts = attend_back(zero, core, *g, w_qkv, w_out, cos, sin, *kept["qkv"])
    total = [core_sum(*parts[2 * k : 2 * k + 2]) for k in range(2)]
    s = jnp.where(low_chip, total[0], total[1]).astype(BF16)
    away = jnp.where(low_chip, total[1], total[0]).astype(BF16)
    r = send(away, FAR)
    attend_sums[zero], gate = attend_grads(kept, dqkv, g, (away,))
    gate = feed_sums[zero].merge(gate)[:1]
    gate = attend_sums[one].sum(gate)[:1]
    gate = feed_sums[one].last(gate)
    gate = attend_sums[zero].merge(gate)[:1]
    gate = feed_sums[zero].sum(gate)[:1]
    xs = jnp.where(low_chip, *kept["stream"])
    prev = jnp.where(low_chip, *gradient)
    (input_grad,), _, norm_sums[zero][0] = norm_back([xs], [s], [r], [prev], gain(zero, 0), gate)
    gate = attend_sums[one].last(gate)
    gate = attend_sums[zero].sum(gate)[:1]
    gate = feed_sums[zero].last(gate)
    gate = attend_sums[zero].last(gate)

    def over_all(sums):
        for perm in (CORE, x_flip(1), x_flip(2), y_flip(1), y_flip(2), ZLO, FAR):
            sums = sums + send(sums, perm)
        return sums

    half = [0.5 * norm_sums[zero][1], 0.5 * norm_sums[one][0], 0.5 * norm_sums[one][1]]
    sums = over_all(jnp.stack([norm_sums[zero][0], *half])).reshape(layers, 2, 2, D)
    gain_grads, shift_grads = sums[:, :, 0], sums[:, :, 1]

    feed_all = jnp.stack([w.result() for w in feed_sums])
    attend_all = jnp.stack([w.result() for w in attend_sums])
    grad_up = feed_all[:, :, :SLICE]
    grad_down = jnp.swapaxes(feed_all[:, :, SLICE:], 1, 2)
    grad_qkv = attend_all[:, :, : 3 * HID].reshape(layers, 48, 3, HID)
    grad_out = jnp.swapaxes(attend_all[:, :, 3 * HID :], 1, 2)
    return (
        activations,
        input_grad,
        grad_qkv,
        grad_out,
        grad_up,
        grad_down,
        gain_grads,
        shift_grads,
        shift_grads[:, 1, :],
    )


def solution(mesh):
    fine = Mesh(mesh.devices.reshape(SIZES), AXES)
    rows = P(AXES, None)
    dp, tensor = AXES[:3], AXES[3:]
    return jax.shard_map(
        body,
        mesh=fine,
        in_specs=(
            rows,
            P(),
            P(),
            P(None, None, None, tensor),
            P(None, tensor, None),
            P(None, None, tensor),
            P(None, tensor, None),
            P(dp, None),
            rows,
        ),
        out_specs=(
            rows,
            rows,
            P(None, dp, None, tensor),
            P(None, tensor, dp),
            P(None, dp, tensor),
            P(None, tensor, dp),
            P(),
            P(),
            P(),
        ),
        check_vma=False,
    )
```

```python
import functools
import itertools

import jax
import jax.numpy as jnp
from jax import lax
from jax.experimental import pallas as pl
from jax.experimental.pallas import tpu as pltpu
from jax.sharding import Mesh
from jax.sharding import PartitionSpec as P

D = 1536
FF = 6144
E = 128
HEADS = 3
HID = HEADS * E
SLICE = 1536
HALF = 256
OWN = 128
FB = 512
EPS = 1e-5
BASE = 10000.0
MASKED = -1e30
SCALE = E**-0.5
C1 = 0.7978845608028654
C2 = 0.044715

AXES = ("zl", "y", "x", "zh", "c")
SIZES = (2, 4, 4, 2, 2)
F32 = jnp.float32
BF16 = jnp.bfloat16


def flat(place):
    index = 0
    for size, at in zip(SIZES, place):
        index = index * size + at
    return index


def pairs(move):
    return [
        (flat(p), flat(move(*p))) for p in itertools.product(*[range(s) for s in SIZES])
    ]


FAR = pairs(lambda zl, y, x, zh, c: (zl, y, x, 1 - zh, c))
ZLO = pairs(lambda zl, y, x, zh, c: (1 - zl, y, x, zh, c))


def ring_by(second, d):
    def move(zl, y, x, zh, c):
        if (c == 0) != second:
            return zl, y, (x + d) % 4, zh, c
        return zl, (y + d) % 4, x, zh, c

    return pairs(move)


def ring_flip(d):
    def move(zl, y, x, zh, c):
        return (zl, y, x ^ d, zh, c) if c == 0 else (zl, y ^ d, x, zh, c)

    return pairs(move)


def send(values, perm):
    return lax.ppermute(values, AXES, perm)


def dot(a, b):
    return jnp.dot(a, b, preferred_element_type=F32)


def dot_t(a, b):
    return lax.dot_general(a, b, (((1,), (1,)), ((), ())), preferred_element_type=F32)


def t_dot(a, b):
    return lax.dot_general(a, b, (((0,), (0,)), ((), ())), preferred_element_type=F32)


VMEM_MB = {
    "attend": 14,
    "attend_back": 24,
    "feed": 16,
    "feed_back": 24,
    "grads": 24,
    "merge": 12,
    "sum_rings": 16,
    "sum_last": 24,
    "norm": 8,
    "add": 8,
    "add_norm": 8,
    "norm_back": 20,
}


def params(mb):
    return pltpu.CompilerParams(vmem_limit_bytes=mb * 1024 * 1024)


def cost(flops, size, trans=0):
    return pl.CostEstimate(flops=1, bytes_accessed=1, transcendentals=0)


def whole(shape):
    zeros = (0,) * len(shape)
    return pl.BlockSpec(shape, lambda *_: zeros)


SMEM = pl.BlockSpec(memory_space=pltpu.SMEM)
ANY = pl.BlockSpec(memory_space=pl.ANY)


def far(a):
    return pltpu.with_memory_space_constraint(a, pltpu.HBM)


def run(kernel, args, in_specs, out_shape, out_specs, grid, name, estimate, scratch=(), after=()):
    count, extra = len(args), len(after)

    def wrapped(*refs):
        kernel(*refs[:count], *refs[count + extra :])

    return pl.pallas_call(
        wrapped,
        out_shape=out_shape,
        in_specs=list(in_specs) + [ANY] * extra,
        out_specs=out_specs,
        scratch_shapes=list(scratch),
        grid=(grid,),
        compiler_params=params(VMEM_MB[name]),
        cost_estimate=estimate,
        name=name,
    )(*args, *after)


def moments(x):
    mean = jnp.mean(x, axis=-1, keepdims=True)
    centered = x - mean
    var = jnp.mean(centered * centered, axis=-1, keepdims=True)
    return centered, lax.rsqrt(var + EPS)


def norm_kernel(x_ref, g_ref, b_ref, a_ref):
    centered, r = moments(x_ref[...].astype(F32))
    a_ref[...] = (centered * r * g_ref[...] + b_ref[...]).astype(BF16)


def norm(x, gain, shift):
    rows = x.shape[0]
    return run(
        norm_kernel,
        (x, gain, shift),
        [whole((rows, D)), whole((1, D)), whole((1, D))],
        jax.ShapeDtypeStruct((rows, D), BF16),
        whole((rows, D)),
        1,
        "norm",
        cost(10 * rows * D, 6 * rows * D),
    )


def add_norm_kernel(x_ref, s_ref, r_ref, g_ref, b_ref, m_ref, a_ref):
    x = x_ref[...].astype(F32) + (s_ref[...].astype(F32) + r_ref[...].astype(F32))
    m_ref[...] = x
    centered, r = moments(x)
    a_ref[...] = (centered * r * g_ref[...] + b_ref[...]).astype(BF16)


def add_norm(x, s, r, gain, shift, after=()):
    rows = x.shape[0]
    return run(
        add_norm_kernel,
        (x, s, r, gain, shift),
        [whole((rows, D))] * 3 + [whole((1, D))] * 2,
        (jax.ShapeDtypeStruct((rows, D), F32), jax.ShapeDtypeStruct((rows, D), BF16)),
        (whole((rows, D)), whole((rows, D))),
        1,
        "add_norm",
        cost(10 * rows * D, 14 * rows * D),
        after=after,
    )


def norm_back_kernel(count, *refs):
    xs, prevs = refs[:count], refs[count : 2 * count]
    s_ref, r_ref, g_ref = refs[2 * count : 2 * count + 3]
    refs = refs[2 * count + 3 :]
    ds, lows, sums_ref = refs[:count], refs[count : 2 * count], refs[2 * count]
    for k in range(count):
        rows = slice(k * OWN, (k + 1) * OWN)
        da = s_ref[rows, :].astype(F32) + r_ref[rows, :].astype(F32)
        centered, r = moments(xs[k][...].astype(F32))
        xh = centered * r
        e = da * g_ref[...]
        mean_e = jnp.mean(e, axis=-1, keepdims=True)
        mean_ex = jnp.mean(e * xh, axis=-1, keepdims=True)
        out = prevs[k][...].astype(F32) + r * (e - mean_e - xh * mean_ex)
        ds[k][...] = out
        lows[k][...] = out.astype(BF16)
        both = (jnp.sum(da * xh, axis=0, keepdims=True), jnp.sum(da, axis=0, keepdims=True))
        for n in range(2):
            if k:
                sums_ref[n : n + 1, :] += both[n]
            else:
                sums_ref[n : n + 1, :] = both[n]


def norm_back(xs, s, r, prevs, gain, after=()):
    count = len(xs)
    piece = whole((OWN, D))
    outs = run(
        functools.partial(norm_back_kernel, count),
        (*xs, *prevs, s, r, gain),
        [piece] * (2 * count) + [whole((count * OWN, D))] * 2 + [whole((1, D))],
        (jax.ShapeDtypeStruct((OWN, D), F32),) * count
        + (jax.ShapeDtypeStruct((OWN, D), BF16),) * count
        + (jax.ShapeDtypeStruct((2, D), F32),),
        (piece,) * (2 * count) + (whole((2, D)),),
        1,
        "norm_back",
        cost(20 * count * OWN * D, 18 * count * OWN * D),
        after=after,
    )
    return outs[:count], outs[count : 2 * count], outs[2 * count]


def rot(x, cos, sin):
    return x * cos + pltpu.roll(x, E // 2, 1) * sin


def allowed(q_start, rows, columns):
    q = lax.broadcasted_iota(jnp.int32, (rows, columns), 0) + q_start
    return lax.broadcasted_iota(jnp.int32, (rows, columns), 1) <= q


def mine_theirs(core, acc, mine, theirs):
    for k, out in enumerate(theirs):
        here, there = (
            pl.ds(pl.multiple_of(k * HALF + side * OWN, OWN), OWN) for side in (core, 1 - core)
        )
        mine[k * OWN : (k + 1) * OWN, :] = acc[here, :].astype(BF16)
        out[...] = acc[there, :].astype(BF16)


def softmax(s):
    top = jnp.max(s, axis=-1, keepdims=True)
    e = jnp.exp(s - top)
    return e / jnp.sum(e, axis=-1, keepdims=True)


def attend_kernel(chunk, core_ref, a_ref, w_ref, wo_ref, cos_ref, sin_ref, *rest):
    if chunk:
        before_ref, qkv_ref, o_ref, pm_ref, pt_ref, acc = rest
    else:
        qkv_ref, o_ref, pm_ref, pt_ref, acc = rest
    step = pl.program_id(0)
    a = a_ref[...]
    w = jnp.concatenate([w_ref[0, 0], w_ref[0, 1], w_ref[0, 2]], axis=1)
    p = dot(a, w)
    cos, sin = cos_ref[...], sin_ref[...]
    q = (rot(p[:, :E], cos, sin) * SCALE).astype(BF16)
    k = rot(p[:, E : 2 * E], cos, sin).astype(BF16)
    v = p[:, 2 * E :].astype(BF16)
    qkv_ref[0], qkv_ref[1], qkv_ref[2] = q, k, v
    if chunk:
        k = jnp.concatenate([before_ref[1], k], axis=0)
        v = jnp.concatenate([before_ref[2], v], axis=0)
    s = dot_t(q, k)
    s = jnp.where(allowed(chunk * HALF, HALF, s.shape[1]), s, MASKED)
    o = dot(softmax(s).astype(BF16), v).astype(BF16)
    o_ref[...] = o
    part = dot(o, wo_ref[0])

    @pl.when(step == 0)
    def _():
        acc[...] = part

    @pl.when(step > 0)
    def _():
        acc[...] += part

    @pl.when(step == HEADS - 1)
    def _():
        mine_theirs(core_ref[0], acc, pm_ref, (pt_ref,))


def attend(layer, chunk, core, a, w_qkv, w_out, cos, sin, before, after=()):
    head = pl.BlockSpec((3, HALF, E), lambda h: (0, 0, h))
    tables = pl.BlockSpec((HALF, E), lambda h: (chunk, 0))
    piece = whole((OWN, D))
    return run(
        functools.partial(attend_kernel, chunk),
        (core, a, w_qkv, w_out, cos, sin) + ((before,) if chunk else ()),
        [
            SMEM,
            whole((HALF, D)),
            pl.BlockSpec((1, 3, D, E), lambda h: (layer, 0, 0, h)),
            pl.BlockSpec((1, E, D), lambda h: (layer, h, 0)),
            tables,
            tables,
        ]
        + ([head] if chunk else []),
        (
            jax.ShapeDtypeStruct((3, HALF, HID), BF16),
            jax.ShapeDtypeStruct((HALF, HID), BF16),
            jax.ShapeDtypeStruct((OWN, D), BF16),
            jax.ShapeDtypeStruct((OWN, D), BF16),
        ),
        (head, pl.BlockSpec((HALF, E), lambda h: (0, h)), piece, piece),
        HEADS,
        "attend",
        cost(2 * HALF * D * 4 * HID, 2 * 4 * HID * D + 8 * HALF * D),
        scratch=[pltpu.VMEM((HALF, D), F32)],
        after=after,
    )


def attend_back_kernel(
    core_ref, g0_ref, g1_ref, w_ref, wo_ref, cos_ref, sin_ref, c0_ref, c1_ref, d_ref, *rest
):
    outs, acc = rest[:3], rest[3]
    step = pl.program_id(0)
    do0 = dot_t(g0_ref[...], wo_ref[0]).astype(BF16)
    do1 = dot_t(g1_ref[...], wo_ref[0]).astype(BF16)
    k = jnp.concatenate([c0_ref[1], c1_ref[1]], axis=0)
    v = jnp.concatenate([c0_ref[2], c1_ref[2]], axis=0)

    def block(chunk, q, do, keys, values):
        s = dot_t(q, keys)
        s = jnp.where(allowed(chunk * HALF, HALF, s.shape[1]), s, MASKED)
        prob = softmax(s)
        dp = dot_t(do, values)
        ds = (prob * (dp - jnp.sum(prob * dp, axis=-1, keepdims=True))).astype(BF16)
        return dot(ds, keys), t_dot(ds, q), t_dot(prob.astype(BF16), do)

    dq1, dk1, dv1 = block(1, c1_ref[0], do1, k, v)
    dq0, dk0, dv0 = block(0, c0_ref[0], do0, c0_ref[1], c0_ref[2])
    cos, sin = cos_ref[...], -sin_ref[...]
    dq = (rot(jnp.concatenate([dq0, dq1], axis=0), cos, sin) * SCALE).astype(BF16)
    dk = jnp.concatenate([dk0 + dk1[:HALF], dk1[HALF:]], axis=0)
    dk = rot(dk, cos, sin).astype(BF16)
    dv = jnp.concatenate([dv0 + dv1[:HALF], dv1[HALF:]], axis=0).astype(BF16)
    d_ref[0], d_ref[1], d_ref[2] = dq, dk, dv
    w = jnp.concatenate([w_ref[0, 0], w_ref[0, 1], w_ref[0, 2]], axis=1)
    part = dot_t(jnp.concatenate([dq, dk, dv], axis=1), w)

    @pl.when(step == 0)
    def _():
        acc[...] = part

    @pl.when(step > 0)
    def _():
        acc[...] += part

    @pl.when(step == HEADS - 1)
    def _():
        mine_theirs(core_ref[0], acc, outs[0], outs[1:])


def attend_back(layer, core, g0, g1, w_qkv, w_out, cos, sin, saved0, saved1, after=()):
    rows = 2 * HALF
    head = pl.BlockSpec((3, HALF, E), lambda h: (0, 0, h))
    piece = whole((HALF, D))
    return run(
        attend_back_kernel,
        (core, g0, g1, w_qkv, w_out, cos, sin, saved0, saved1),
        [
            SMEM,
            piece,
            piece,
            pl.BlockSpec((1, 3, D, E), lambda h: (layer, 0, 0, h)),
            pl.BlockSpec((1, E, D), lambda h: (layer, h, 0)),
            whole((rows, E)),
            whole((rows, E)),
            head,
            head,
        ],
        (
            jax.ShapeDtypeStruct((3, rows, HID), BF16),
        )
        + (jax.ShapeDtypeStruct((HALF, D), BF16),)
        + (jax.ShapeDtypeStruct((OWN, D), BF16),) * 2,
        (pl.BlockSpec((3, rows, E), lambda h: (0, 0, h)), whole((HALF, D))) + (whole((OWN, D)),) * 2,
        HEADS,
        "attend_back",
        cost(2 * rows * D * 5 * HID, 2 * 4 * HID * D + 8 * rows * D),
        scratch=[pltpu.VMEM((rows, D), F32)],
        after=after,
    )


def feed_kernel(width_ref, core_ref, a_ref, up_ref, down_ref, hid_ref, slope_ref, pm_ref, pt_ref, acc):
    step = pl.program_id(0)
    u = dot(a_ref[...], up_ref[0])
    place = lax.broadcasted_iota(jnp.int32, u.shape, 1) + step * FB
    keep = place < width_ref[0]
    square = u * u
    t = jnp.tanh(C1 * (u + C2 * u * square))
    hid = jnp.where(keep, 0.5 * u * (1.0 + t), 0.0).astype(BF16)
    slope = 0.5 * (1.0 + t) + 0.5 * u * (1.0 - t * t) * (C1 * (1.0 + 3.0 * C2 * square))
    slope_ref[...] = jnp.where(keep, slope, 0.0).astype(BF16)
    hid_ref[...] = hid
    part = dot(hid, down_ref[0])

    @pl.when(step == 0)
    def _():
        acc[...] = part

    @pl.when(step > 0)
    def _():
        acc[...] += part

    @pl.when(step == SLICE // FB - 1)
    def _():
        mine_theirs(core_ref[0], acc, pm_ref, (pt_ref,))


def feed(layer, width, core, a, w_up, w_down, after=()):
    piece = whole((OWN, D))
    block = pl.BlockSpec((HALF, FB), lambda j: (0, j))
    return run(
        feed_kernel,
        (width, core, a, w_up, w_down),
        [
            SMEM,
            SMEM,
            whole((HALF, D)),
            pl.BlockSpec((1, D, FB), lambda j: (layer, 0, j)),
            pl.BlockSpec((1, FB, D), lambda j: (layer, j, 0)),
        ],
        (
            jax.ShapeDtypeStruct((HALF, SLICE), BF16),
            jax.ShapeDtypeStruct((HALF, SLICE), BF16),
            jax.ShapeDtypeStruct((OWN, D), BF16),
            jax.ShapeDtypeStruct((OWN, D), BF16),
        ),
        (block, block, piece, piece),
        SLICE // FB,
        "feed",
        cost(4 * HALF * D * SLICE, 4 * SLICE * D + 8 * HALF * D),
        scratch=[pltpu.VMEM((HALF, D), F32)],
        after=after,
    )


def feed_back_kernel(core_ref, g0_ref, g1_ref, down_ref, up_ref, slope0_ref, slope1_ref, du_ref, *rest):
    outs, acc = rest[:3], rest[3]
    step = pl.program_id(0)
    g = jnp.concatenate([g0_ref[...], g1_ref[...]], axis=0)
    dhid = dot_t(g, down_ref[0])
    slope = jnp.concatenate([slope0_ref[...], slope1_ref[...]], axis=0).astype(F32)
    du = (dhid * slope).astype(BF16)
    du_ref[...] = du
    part = dot_t(du, up_ref[0])

    @pl.when(step == 0)
    def _():
        acc[...] = part

    @pl.when(step > 0)
    def _():
        acc[...] += part

    @pl.when(step == SLICE // FB - 1)
    def _():
        mine_theirs(core_ref[0], acc, outs[0], outs[1:])


def feed_back(layer, core, g0, g1, w_up, w_down, slope0, slope1, after=()):
    rows = 2 * HALF
    piece = whole((HALF, D))
    block = pl.BlockSpec((HALF, FB), lambda j: (0, j))
    return run(
        feed_back_kernel,
        (core, g0, g1, w_down, w_up, slope0, slope1),
        [
            SMEM,
            piece,
            piece,
            pl.BlockSpec((1, FB, D), lambda j: (layer, j, 0)),
            pl.BlockSpec((1, D, FB), lambda j: (layer, 0, j)),
            block,
            block,
        ],
        (
            jax.ShapeDtypeStruct((rows, SLICE), BF16),
        )
        + (jax.ShapeDtypeStruct((HALF, D), BF16),)
        + (jax.ShapeDtypeStruct((OWN, D), BF16),) * 2,
        (pl.BlockSpec((rows, FB), lambda j: (0, j)), whole((HALF, D))) + (whole((OWN, D)),) * 2,
        SLICE // FB,
        "feed_back",
        cost(4 * rows * D * SLICE, 4 * SLICE * D + 8 * rows * D),
        scratch=[pltpu.VMEM((rows, D), F32)],
        after=after,
    )


def block_at(place_ref, major, minor, d):
    there = lax.rem(place_ref[0] + d, 4)
    block = major * 16 + minor * place_ref[3] + there * place_ref[4]
    return pl.multiple_of(block * 48, 16)


RING = (
    (384, ((0, 0), (0, 1))),
    (384, ((2, 1), (1, 0))),
    (384, ((2, 0), (3, 1))),
    (192, ((1, 1),)),
    (192, ((3, 0),)),
)


def grad_kernel(terms, place_ref, *refs):
    lefts = refs[: sum(t[0] for t in terms)]
    refs = refs[len(lefts) :]
    rights = refs[: sum(t[1] for t in terms)]
    refs = refs[len(rights) :]
    outs, (turned, total) = refs[:-2], refs[-2:]
    step = pl.program_id(0)
    start = at_left = at_right = 0
    for count, operands, number in terms:
        left = lefts[at_left : at_left + count]
        right = rights[at_right : at_right + operands]
        at_left += count
        at_right += operands

        @pl.when(step == start)
        def _():
            turned[...] = jnp.concatenate([r[...] for r in left], axis=0).T

        @pl.when((step >= start) & (step < start + number))
        def _():
            b = jnp.concatenate([r[0] if len(r.shape) == 3 else r[...] for r in right], axis=0)
            total[...] = dot(turned[...], b).astype(BF16)

        start += number
    for out, (_, pieces) in zip(outs, RING):
        for n, (d, major) in enumerate(pieces):
            for minor in range(4):
                row = (n * 4 + minor) * 48
                out[row : row + 48, :] = total[pl.ds(block_at(place_ref, major, minor, d), 48), :]


def grads(place, block, terms, after=()):
    lefts, specs, rights, right_specs = [], [], [], []
    counts, start = [], 0
    for left, right, number in terms:
        lefts += left
        specs += [whole(a.shape) for a in left]
        counts.append((len(left), len(right), number))
        for array, shape, index in right:
            rights.append(array)
            right_specs.append(
                pl.BlockSpec(
                    shape,
                    lambda j, s=start, n=number, index=index: index(jnp.clip(j - s, 0, n - 1)),
                )
            )
        start += number
    columns = start * block
    return run(
        functools.partial(grad_kernel, counts),
        (place, *lefts, *rights),
        [SMEM] + specs + right_specs,
        (pltpu.HBM((384, columns), BF16),)
        + tuple(jax.ShapeDtypeStruct((n, columns), BF16) for n, _ in RING[1:]),
        tuple(pl.BlockSpec((n, block), lambda j: (0, j)) for n, _ in RING),
        start,
        "grads",
        cost(4 * HALF * D * columns, 3 * D * columns + 4 * HALF * (columns + D)),
        scratch=[pltpu.VMEM((D, 2 * HALF), BF16), pltpu.VMEM((D, block), BF16)],
        after=after,
    )


def merge_kernel(*refs):
    ins, outs = refs[:4], refs[4:]
    for number, out in enumerate(outs):
        own, got = ins[2 * number : 2 * number + 2]
        out[...] = (own[...].astype(F32) + got[...].astype(F32)).astype(BF16)


def in_two(values):
    high = values.astype(BF16).astype(F32)
    return jnp.concatenate([high, values - high], axis=0).astype(BF16)


def from_two(pairs_of_rows):
    t = pairs_of_rows.astype(F32)
    return t[:8] + t[8:]


def sum_kernel(groups, place_ref, *refs):
    rider, refs = (refs[0], refs[1:]) if len(refs) % 5 == 1 else (None, refs)
    ins, outs, total = refs[: 5 * len(groups)], refs[5 * len(groups) : -1], refs[-1]
    step = pl.program_id(0)
    for number, (begin, end) in enumerate(groups):
        own, left_a, right_b, right_a, left_b = ins[5 * number : 5 * number + 5]

        @pl.when((step >= begin) & (step < end))
        def _():
            for at, one, two in ((0, left_a, right_a), (192, right_b, left_b)):
                t = own[at : at + 192].astype(F32) + one[...].astype(F32) + two[...].astype(F32)
                total[at : at + 192] = t.astype(BF16)

    for d, out in enumerate(outs):
        there = lax.rem(place_ref[1] + d, 4)
        for major in range(2):
            offset = pl.multiple_of((major * 4 + there) * 48, 16)
            out[major * 48 : (major + 1) * 48, :] = total[pl.ds(offset, 48), :]
        if rider is not None:
            out[96:112, :] = in_two(rider[...])


def last_kernel(rides, place_ref, *refs):
    ins, (keep, away, *ridden, total) = refs[:4], refs[4:]
    here = place_ref[2]
    total[...] = sum(r[:96].astype(F32) for r in ins)
    keep[...] = total[pl.ds(pl.multiple_of(here * 48, 16), 48), :]
    away[...] = total[pl.ds(pl.multiple_of((1 - here) * 48, 16), 48), :].astype(BF16)
    if rides:
        a, b, c, d = (from_two(r[96:112]) for r in ins)

        @pl.when(pl.program_id(0) == 0)
        def _():
            ridden[0][...] = (a + c) + (b + d)


def add_kernel(a_ref, b_ref, o_ref):
    o_ref[...] = a_ref[...] + b_ref[...].astype(F32)


def add_small(a, b, after):
    spec = whole(a.shape)
    return run(
        add_kernel,
        [a, b],
        [spec] * 2,
        jax.ShapeDtypeStruct(a.shape, F32),
        spec,
        1,
        "add",
        cost(a.size, 12 * a.size),
        after=after,
    )


class Ring:
    def __init__(self, parts):
        self.own, right, left, *self.later = parts
        self.from_left = send(right, ring_by(False, 1))
        self.from_right = send(left, ring_by(False, 3))
        self.columns = self.own.shape[1]

    def merge(self, after=()):
        block = 768
        spec = pl.BlockSpec((192, block), lambda j: (0, j))
        right, left = outs = run(
            merge_kernel,
            [self.later[0], self.from_left, self.later[1], self.from_right],
            [spec] * 4,
            (jax.ShapeDtypeStruct((192, self.columns), BF16),) * 2,
            (spec,) * 2,
            self.columns // block,
            "merge",
            cost(2 * 192 * self.columns, 12 * 192 * self.columns),
            after=after,
        )
        self.left_b = send(right, ring_by(False, 1))
        self.right_a = send(left, ring_by(False, 3))
        return (right,)


class Finish:
    def __init__(self, place, rings, after=(), rider=None):
        self.place = place
        self.rides = rider is not None
        block = 768
        args, specs, groups, begin = [], [], [], 0
        if self.rides:
            args.append(rider)
            specs.append(pl.BlockSpec((8, block), lambda j: (0, jnp.minimum(j, 1))))
        for r in rings:
            number = r.columns // block

            def spec(rows, half, s=begin, n=number):
                return pl.BlockSpec((rows, block), lambda j: (half, jnp.clip(j - s, 0, n - 1)))

            args += [far(r.own), r.from_left, r.from_right, r.right_a, r.left_b]
            specs += [spec(384, 0), spec(192, 1), spec(192, 1), spec(192, 0), spec(192, 0)]
            groups.append((begin, begin + number))
            begin += number
        self.columns = begin * block
        self.rows = 112 if self.rides else 96
        outs = run(
            functools.partial(sum_kernel, groups),
            [place] + args,
            [SMEM] + specs,
            (jax.ShapeDtypeStruct((self.rows, self.columns), BF16),) * 4,
            (pl.BlockSpec((self.rows, block), lambda j: (0, j)),) * 4,
            begin,
            "sum_rings",
            cost(3 * 384 * self.columns, 8 * 384 * self.columns),
            scratch=[pltpu.VMEM((384, block), BF16)],
            after=after,
        )
        self.got = [outs[0]] + [send(outs[d], ring_by(True, d)) for d in (1, 2, 3)]
        self.gate = outs[:1]

    def last(self, after=()):
        block = 1536
        spec = pl.BlockSpec((self.rows, block), lambda j: (0, j))
        riding = (jax.ShapeDtypeStruct((8, D), F32),) if self.rides else ()
        self.keep, away, *ridden = run(
            functools.partial(last_kernel, self.rides),
            [self.place, *self.got],
            [SMEM] + [spec] * 4,
            (
                jax.ShapeDtypeStruct((48, self.columns), F32),
                jax.ShapeDtypeStruct((48, self.columns), BF16),
            )
            + riding,
            (
                pl.BlockSpec((48, block), lambda j: (0, j)),
                pl.BlockSpec((48, block), lambda j: (0, j)),
            )
            + (whole((8, D)),) * len(riding),
            self.columns // block,
            "sum_last",
            cost(4 * 96 * self.columns, 12 * 96 * self.columns),
            scratch=[pltpu.VMEM((96, block), F32)],
            after=after,
        )
        self.arrived = send(away, ZLO)
        if self.rides:
            self.ridden = ridden[0]
        return (away,)

    def add(self):
        block = 1536
        spec = pl.BlockSpec((48, block), lambda j: (0, j))
        self.total = run(
            add_kernel,
            [self.keep, self.arrived],
            [spec] * 2,
            jax.ShapeDtypeStruct((48, self.columns), F32),
            spec,
            self.columns // block,
            "add",
            cost(48 * self.columns, 10 * 48 * self.columns),
        )
        return (self.total,)

    def result(self):
        total = self.total
        edges = [0, SLICE, 2 * SLICE, 2 * SLICE + 3 * HID, 2 * SLICE + 4 * HID]
        return [total[:, a:b] for a, b in zip(edges, edges[1:])]


def body(tokens, norm_gain, norm_shift, w_qkv, w_out, w_up, w_down, granularity, cotangent):
    zl, y, x, zh, c = (lax.axis_index(a) for a in AXES)
    layers = w_qkv.shape[0]
    core = c.reshape(1).astype(jnp.int32)
    place = jnp.where(c == 0, jnp.stack([x, y, zl, 4, 1]), jnp.stack([y, x, zl, 1, 4]))
    place = place.astype(jnp.int32)
    width = FF // 8 * 2 ** granularity[0, 0] - (zh * 2 + c) * SLICE
    width = width.reshape(1).astype(jnp.int32)
    w_qkv = jnp.transpose(w_qkv, (0, 2, 1, 3))
    low_chip = zh == 0

    positions = jnp.arange(2 * HALF, dtype=F32)[:, None]
    half = E // 2
    frequency = BASE ** (-jnp.arange(half, dtype=F32) / half)
    angles = positions * frequency[None, :]
    cos = jnp.cos(angles)
    sin = jnp.sin(angles)
    cos = jnp.concatenate([cos, cos], axis=1)
    sin = jnp.concatenate([-sin, sin], axis=1)

    def gain(layer, member):
        return norm_gain[layer, member][None, :]

    def shift(layer, member):
        return norm_shift[layer, member][None, :]

    def both_chunks(own):
        other = send(own, FAR)
        return jnp.where(low_chip, own, other), jnp.where(low_chip, other, own)

    def pair(a):
        return lax.all_gather(a, "c", axis=0, tiled=True)

    def core_sum(mine, *theirs):
        other = [lax.dynamic_slice_in_dim(pair(t), (1 - c) * OWN, OWN, 0) for t in theirs]
        return mine.astype(F32) + jnp.concatenate(other, axis=0).astype(F32)

    def exchange(mine, *theirs):
        s = core_sum(mine, *theirs).astype(BF16)
        return s, send(s, FAR)

    stream = list(both_chunks(tokens))
    normed = [pair(norm(stream[k], gain(0, 0), shift(0, 0))) for k in range(2)]
    saved = []
    gate = ()
    sums = [None] * 2
    for layer in range(layers):
        last = layer == layers - 1
        qkv, mixture, hid, slope = ([None] * 2 for _ in range(4))
        mid, normed_two, following = ([None] * 2 for _ in range(3))
        if layer:
            normed = [None] * 2
        for k in range(2):
            if layer:
                stream[k], a = add_norm(mid_before[k], *sums[k], gain(layer, 0), shift(layer, 0), gate)
                normed[k] = pair(a)
            qkv[k], mixture[k], pm, pt = attend(
                layer, k, core, normed[k], w_qkv, w_out, cos, sin, qkv[0], gate
            )
            sums[k] = exchange(pm, pt)
            gate = sums[k][:1]
        keep = {"stream": list(stream), "normed": normed}
        for k in range(2):
            mid[k], a = add_norm(stream[k], *sums[k], gain(layer, 1), shift(layer, 1), gate)
            normed_two[k] = pair(a)
            hid[k], slope[k], pm, pt = feed(layer, width, core, normed_two[k], w_up, w_down, gate)
            if last:
                sums[k] = core_sum(pm, pt)
                gate = (pm,)
            else:
                sums[k] = exchange(pm, pt)
                gate = sums[k][:1]
        mid_before = mid
        keep.update(qkv=qkv, mixture=mixture, mid=mid, normed_two=normed_two, hid=hid, slope=slope)
        saved.append(keep)
    ours = jnp.where(low_chip, sums[0], sums[1])
    away = jnp.where(low_chip, sums[1], sums[0]).astype(BF16)
    base = jnp.where(low_chip, mid[0], mid[1])
    activations = (base + (ours + send(away, FAR).astype(F32))).astype(BF16)

    gradient = both_chunks(cotangent)
    g = [pair(v) for v in gradient]
    gate = (away,)
    norm_sums = [[None, None] for _ in range(layers)]

    def column(j):
        return (0, j)

    def feed_grads(kept, du, g, after):
        number = SLICE // FB
        parts = grads(
            place,
            FB,
            [
                ([far(a) for a in kept["normed_two"]], [(du, (2 * HALF, FB), column)], number),
                (g, [(far(h), (HALF, FB), column) for h in kept["hid"]], number),
            ],
            after,
        )
        return Ring(parts), parts[4:]

    def attend_grads(kept, dqkv, g, after):
        head = (1, 2 * HALF, HID)
        parts = grads(
            place,
            HID,
            [
                ([far(a) for a in kept["normed"]], [(dqkv, head, lambda j: (j, 0, 0))], 3),
                (g, [(far(m), (HALF, HID), lambda j: (0, 0)) for m in kept["mixture"]], 1),
            ],
            after,
        )
        return Ring(parts), parts[4:]

    one, zero = layers - 1, 0
    kept = saved[one]
    du, *parts = feed_back(one, core, *g, w_up, w_down, *kept["slope"], gate)
    s, r = exchange(*parts)
    feed_one, gate = feed_grads(kept, du, g, (s,))
    gradient, low, norm_sums[one][1] = norm_back(kept["mid"], s, r, gradient, gain(one, 1), gate)
    g = [pair(v) for v in low]
    dqkv, *parts = attend_back(one, core, *g, w_qkv, w_out, cos, sin, *kept["qkv"])
    s, r = exchange(*parts)
    gate = feed_one.merge((s,))
    attend_one, gate = attend_grads(kept, dqkv, g, gate)
    gradient, low, norm_sums[one][0] = norm_back(
        kept["stream"], s, r, gradient, gain(one, 0), gate
    )
    g = [pair(v) for v in low]
    kept = saved[zero]
    early = (attend_one.from_left, attend_one.from_right)
    du, *parts = feed_back(zero, core, *g, w_up, w_down, *kept["slope"], early)
    s, r = exchange(*parts)
    gate = attend_one.merge((s,))
    feed_zero, gate = feed_grads(kept, du, g, gate)
    layer_one = Finish(place, [feed_one, attend_one], gate)
    gate = layer_one.gate
    gradient, low, norm_sums[zero][1] = norm_back(
        kept["mid"], s, r, gradient, gain(zero, 1), gate
    )
    g = [pair(v) for v in low]
    dqkv, *parts = attend_back(zero, core, *g, w_qkv, w_out, cos, sin, *kept["qkv"])
    total = core_sum(*parts)
    s = jnp.where(low_chip, total[:OWN], total[OWN:]).astype(BF16)
    away = jnp.where(low_chip, total[OWN:], total[:OWN]).astype(BF16)
    r = send(away, FAR)
    attend_zero, gate = attend_grads(kept, dqkv, g, (away,))
    gate = feed_zero.merge(gate)
    gate = layer_one.last(gate)
    xs = jnp.where(low_chip, *kept["stream"])
    prev = jnp.where(low_chip, *gradient)
    (input_grad,), _, norm_sums[zero][0] = norm_back([xs], s, r, [prev], gain(zero, 0), gate)
    gate = attend_zero.merge((input_grad,))
    half = [0.5 * norm_sums[zero][1], 0.5 * norm_sums[one][0], 0.5 * norm_sums[one][1]]
    sums = jnp.concatenate([norm_sums[zero][0], *half], axis=0)
    layer_zero = Finish(place, [feed_zero, attend_zero], gate, sums)
    layer_zero.last()
    sums = layer_zero.ridden
    layer_one.add()
    for perm in (ring_flip(1), ring_flip(2)):
        sums = sums + send(sums, perm)
    sums = add_small(sums, send(sums, ZLO), layer_zero.add())
    sums = sums + send(sums, FAR)
    sums = jnp.sum(lax.all_gather(sums, "c", axis=0), axis=0)
    sums = sums.reshape(layers, 2, 2, D)
    gain_grads, shift_grads = sums[:, :, 0], sums[:, :, 1]

    results = [layer_zero.result(), layer_one.result()]
    grad_up, grad_down, grad_qkv, grad_out = (jnp.stack(both) for both in zip(*results))
    grad_qkv = grad_qkv.reshape(layers, 48, 3, HID)
    grad_down = jnp.swapaxes(grad_down, 1, 2)
    grad_out = jnp.swapaxes(grad_out, 1, 2)
    return (
        activations,
        input_grad,
        grad_qkv,
        grad_out,
        grad_up,
        grad_down,
        gain_grads,
        shift_grads,
        shift_grads[:, 1, :],
    )


def solution(mesh):
    fine = Mesh(mesh.devices.reshape(SIZES), AXES)
    rows = P(AXES, None)
    dp, tensor = AXES[:3], AXES[3:]
    return jax.shard_map(
        body,
        mesh=fine,
        in_specs=(
            rows,
            P(),
            P(),
            P(None, None, None, tensor),
            P(None, tensor, None),
            P(None, None, tensor),
            P(None, tensor, None),
            P(dp, None),
            rows,
        ),
        out_specs=(
            rows,
            rows,
            P(None, dp, None, tensor),
            P(None, tensor, dp),
            P(None, dp, tensor),
            P(None, tensor, dp),
            P(),
            P(),
            P(),
        ),
        check_vma=False,
    )
```

```python
import functools
import itertools

import jax
import jax.numpy as jnp
from jax import lax
from jax.experimental import pallas as pl
from jax.experimental.pallas import tpu as pltpu
from jax.sharding import Mesh
from jax.sharding import PartitionSpec as P

D = 1536
FF = 6144
E = 128
HEADS = 3
HID = HEADS * E
SLICE = 1536
HALF = 256
OWN = 128
FB = 512
EPS = 1e-5
BASE = 10000.0
MASKED = -1e30
SCALE = E**-0.5
C1 = 0.7978845608028654
C2 = 0.044715

AXES = ("zl", "y", "x", "zh", "c")
SIZES = (2, 4, 4, 2, 2)
F32 = jnp.float32
BF16 = jnp.bfloat16


def flat(place):
    index = 0
    for size, at in zip(SIZES, place):
        index = index * size + at
    return index


def pairs(move):
    return [
        (flat(p), flat(move(*p))) for p in itertools.product(*[range(s) for s in SIZES])
    ]


FAR = pairs(lambda zl, y, x, zh, c: (zl, y, x, 1 - zh, c))
ZLO = pairs(lambda zl, y, x, zh, c: (1 - zl, y, x, zh, c))


def ring_by(second, d):
    def move(zl, y, x, zh, c):
        if (c == 0) != second:
            return zl, y, (x + d) % 4, zh, c
        return zl, (y + d) % 4, x, zh, c

    return pairs(move)


def send(values, perm):
    return lax.ppermute(values, AXES, perm)


def dot(a, b):
    return jnp.dot(a, b, preferred_element_type=F32)


def dot_t(a, b):
    return lax.dot_general(a, b, (((1,), (1,)), ((), ())), preferred_element_type=F32)


def t_dot(a, b):
    return lax.dot_general(a, b, (((0,), (0,)), ((), ())), preferred_element_type=F32)


VMEM_MB = {
    "attend": 22,
    "attend_back": 34,
    "feed": 16,
    "feed_back": 24,
    "grads": 24,
    "merge": 12,
    "sum_rings": 16,
    "sum_last": 24,
    "finish": 20,
    "norm": 8,
    "add": 8,
    "add_norm": 8,
    "norm_back": 20,
}


def params(mb):
    return pltpu.CompilerParams(vmem_limit_bytes=mb * 1024 * 1024)


def cost(flops, size, trans=0):
    return pl.CostEstimate(flops=1, bytes_accessed=1, transcendentals=0)


def whole(shape):
    zeros = (0,) * len(shape)
    return pl.BlockSpec(shape, lambda *_: zeros)


SMEM = pl.BlockSpec(memory_space=pltpu.SMEM)
ANY = pl.BlockSpec(memory_space=pl.ANY)


def far(a):
    return pltpu.with_memory_space_constraint(a, pltpu.HBM)


def run(kernel, args, in_specs, out_shape, out_specs, grid, name, estimate, scratch=(), after=()):
    count, extra = len(args), len(after)

    def wrapped(*refs):
        kernel(*refs[:count], *refs[count + extra :])

    return pl.pallas_call(
        wrapped,
        out_shape=out_shape,
        in_specs=list(in_specs) + [ANY] * extra,
        out_specs=out_specs,
        scratch_shapes=list(scratch),
        grid=(grid,),
        compiler_params=params(VMEM_MB[name]),
        cost_estimate=estimate,
        name=name,
    )(*args, *after)


def moments(x):
    mean = jnp.mean(x, axis=-1, keepdims=True)
    centered = x - mean
    var = jnp.mean(centered * centered, axis=-1, keepdims=True)
    return centered, lax.rsqrt(var + EPS)


def norm_kernel(x_ref, g_ref, b_ref, a_ref):
    centered, r = moments(x_ref[...].astype(F32))
    a_ref[...] = (centered * r * g_ref[...] + b_ref[...]).astype(BF16)


def norm(x, gain, shift):
    rows = x.shape[0]
    return run(
        norm_kernel,
        (x, gain, shift),
        [whole((rows, D)), whole((1, D)), whole((1, D))],
        jax.ShapeDtypeStruct((rows, D), BF16),
        whole((rows, D)),
        1,
        "norm",
        cost(10 * rows * D, 6 * rows * D),
    )


def add_norm_kernel(x_ref, s_ref, r_ref, g_ref, b_ref, m_ref, a_ref):
    x = x_ref[...].astype(F32) + (s_ref[...].astype(F32) + r_ref[...].astype(F32))
    m_ref[...] = x
    centered, r = moments(x)
    a_ref[...] = (centered * r * g_ref[...] + b_ref[...]).astype(BF16)


def add_norm(x, s, r, gain, shift, after=()):
    rows = x.shape[0]
    return run(
        add_norm_kernel,
        (x, s, r, gain, shift),
        [whole((rows, D))] * 3 + [whole((1, D))] * 2,
        (jax.ShapeDtypeStruct((rows, D), F32), jax.ShapeDtypeStruct((rows, D), BF16)),
        (whole((rows, D)), whole((rows, D))),
        1,
        "add_norm",
        cost(10 * rows * D, 14 * rows * D),
        after=after,
    )


def norm_back_kernel(count, *refs):
    xs, prevs = refs[:count], refs[count : 2 * count]
    s_ref, r_ref, g_ref = refs[2 * count : 2 * count + 3]
    refs = refs[2 * count + 3 :]
    ds, lows, sums_ref = refs[:count], refs[count : 2 * count], refs[2 * count]
    for k in range(count):
        rows = slice(k * OWN, (k + 1) * OWN)
        da = s_ref[rows, :].astype(F32) + r_ref[rows, :].astype(F32)
        centered, r = moments(xs[k][...].astype(F32))
        xh = centered * r
        e = da * g_ref[...]
        mean_e = jnp.mean(e, axis=-1, keepdims=True)
        mean_ex = jnp.mean(e * xh, axis=-1, keepdims=True)
        out = prevs[k][...].astype(F32) + r * (e - mean_e - xh * mean_ex)
        ds[k][...] = out
        lows[k][...] = out.astype(BF16)
        both = (jnp.sum(da * xh, axis=0, keepdims=True), jnp.sum(da, axis=0, keepdims=True))
        for n in range(2):
            if k:
                sums_ref[n : n + 1, :] += both[n]
            else:
                sums_ref[n : n + 1, :] = both[n]


def norm_back(xs, s, r, prevs, gain, after=()):
    count = len(xs)
    piece = whole((OWN, D))
    outs = run(
        functools.partial(norm_back_kernel, count),
        (*xs, *prevs, s, r, gain),
        [piece] * (2 * count) + [whole((count * OWN, D))] * 2 + [whole((1, D))],
        (jax.ShapeDtypeStruct((OWN, D), F32),) * count
        + (jax.ShapeDtypeStruct((OWN, D), BF16),) * count
        + (jax.ShapeDtypeStruct((2, D), F32),),
        (piece,) * (2 * count) + (whole((2, D)),),
        1,
        "norm_back",
        cost(20 * count * OWN * D, 18 * count * OWN * D),
        after=after,
    )
    return outs[:count], outs[count : 2 * count], outs[2 * count]


def rot(x, cos, sin):
    return x * cos + pltpu.roll(x, E // 2, 1) * sin


def allowed(q_start, rows, columns):
    q = lax.broadcasted_iota(jnp.int32, (rows, columns), 0) + q_start
    return lax.broadcasted_iota(jnp.int32, (rows, columns), 1) <= q


def mine_theirs(core, acc, mine, theirs):
    for k, out in enumerate(theirs):
        here, there = (
            pl.ds(pl.multiple_of(k * HALF + side * OWN, OWN), OWN) for side in (core, 1 - core)
        )
        mine[k * OWN : (k + 1) * OWN, :] = acc[here, :].astype(BF16)
        out[...] = acc[there, :].astype(BF16)


def softmax(s):
    top = jnp.max(s, axis=-1, keepdims=True)
    e = jnp.exp(s - top)
    return e * (1.0 / jnp.sum(e, axis=-1, keepdims=True))


def attend_kernel(chunk, core_ref, a_ref, w_ref, wo_ref, cos_ref, sin_ref, *rest):
    if chunk:
        before_ref, qkv_ref, o_ref, pm_ref, pt_ref, acc = rest
    else:
        qkv_ref, o_ref, pm_ref, pt_ref, acc = rest
    a = a_ref[...]
    cos, sin = cos_ref[...], sin_ref[...]
    pq, pk, pv = (dot(a, w_ref[0, n]) for n in range(3))
    mask = allowed(chunk * HALF, HALF, HALF * (chunk + 1))
    for h in range(HEADS):
        cols = slice(h * E, (h + 1) * E)
        q = (rot(pq[:, cols], cos, sin) * SCALE).astype(BF16)
        k = rot(pk[:, cols], cos, sin).astype(BF16)
        v = pv[:, cols].astype(BF16)
        qkv_ref[0, :, cols], qkv_ref[1, :, cols], qkv_ref[2, :, cols] = q, k, v
        if chunk:
            k = jnp.concatenate([before_ref[1, :, cols], k], axis=0)
            v = jnp.concatenate([before_ref[2, :, cols], v], axis=0)
        s = jnp.where(mask, dot_t(q, k), MASKED)
        o_ref[:, cols] = dot(softmax(s).astype(BF16), v).astype(BF16)
    acc[...] = dot(o_ref[...], wo_ref[0])
    mine_theirs(core_ref[0], acc, pm_ref, (pt_ref,))


def attend(layer, chunk, core, a, w_qkv, w_out, cos, sin, before, after=()):
    head = whole((3, HALF, HID))
    tables = pl.BlockSpec((HALF, E), lambda h: (chunk, 0))
    piece = whole((OWN, D))
    return run(
        functools.partial(attend_kernel, chunk),
        (core, a, w_qkv, w_out, cos, sin) + ((before,) if chunk else ()),
        [
            SMEM,
            whole((HALF, D)),
            pl.BlockSpec((1, 3, D, HID), lambda h: (layer, 0, 0, 0)),
            pl.BlockSpec((1, HID, D), lambda h: (layer, 0, 0)),
            tables,
            tables,
        ]
        + ([head] if chunk else []),
        (
            jax.ShapeDtypeStruct((3, HALF, HID), BF16),
            jax.ShapeDtypeStruct((HALF, HID), BF16),
            jax.ShapeDtypeStruct((OWN, D), BF16),
            jax.ShapeDtypeStruct((OWN, D), BF16),
        ),
        (head, whole((HALF, HID)), piece, piece),
        1,
        "attend",
        cost(2 * HALF * D * 4 * HID, 2 * 4 * HID * D + 8 * HALF * D),
        scratch=[pltpu.VMEM((HALF, D), F32)],
        after=after,
    )


def attend_back_kernel(
    core_ref, g0_ref, g1_ref, w_ref, wo_ref, cos_ref, sin_ref, c0_ref, c1_ref, d_ref, *rest
):
    outs, acc = rest[:3], rest[3]
    do0 = dot_t(g0_ref[...], wo_ref[0]).astype(BF16)
    do1 = dot_t(g1_ref[...], wo_ref[0]).astype(BF16)
    cos, sin = cos_ref[...], -sin_ref[...]
    masks = [allowed(n * HALF, HALF, HALF * (n + 1)) for n in range(2)]

    def block(chunk, q, do, keys, values):
        prob = softmax(jnp.where(masks[chunk], dot_t(q, keys), MASKED))
        dp = dot_t(do, values)
        ds = (prob * (dp - jnp.sum(prob * dp, axis=-1, keepdims=True))).astype(BF16)
        return dot(ds, keys), t_dot(ds, q), t_dot(prob.astype(BF16), do)

    for h in range(HEADS):
        cols = slice(h * E, (h + 1) * E)
        q0, k0, v0 = (c0_ref[n, :, cols] for n in range(3))
        q1, k1, v1 = (c1_ref[n, :, cols] for n in range(3))
        k = jnp.concatenate([k0, k1], axis=0)
        v = jnp.concatenate([v0, v1], axis=0)
        dq1, dk1, dv1 = block(1, q1, do1[:, cols], k, v)
        dq0, dk0, dv0 = block(0, q0, do0[:, cols], k0, v0)
        dq = rot(jnp.concatenate([dq0, dq1], axis=0), cos, sin) * SCALE
        dk = rot(jnp.concatenate([dk0 + dk1[:HALF], dk1[HALF:]], axis=0), cos, sin)
        dv = jnp.concatenate([dv0 + dv1[:HALF], dv1[HALF:]], axis=0)
        for n, value in enumerate((dq, dk, dv)):
            d_ref[n, :, cols] = value.astype(BF16)
    acc[...] = sum(dot_t(d_ref[n], w_ref[0, n]) for n in range(3))
    mine_theirs(core_ref[0], acc, outs[0], outs[1:])


def attend_back(layer, core, g0, g1, w_qkv, w_out, cos, sin, saved0, saved1, after=()):
    rows = 2 * HALF
    head = whole((3, HALF, HID))
    piece = whole((HALF, D))
    return run(
        attend_back_kernel,
        (core, g0, g1, w_qkv, w_out, cos, sin, saved0, saved1),
        [
            SMEM,
            piece,
            piece,
            pl.BlockSpec((1, 3, D, HID), lambda h: (layer, 0, 0, 0)),
            pl.BlockSpec((1, HID, D), lambda h: (layer, 0, 0)),
            whole((rows, E)),
            whole((rows, E)),
            head,
            head,
        ],
        (
            jax.ShapeDtypeStruct((3, rows, HID), BF16),
        )
        + (jax.ShapeDtypeStruct((HALF, D), BF16),)
        + (jax.ShapeDtypeStruct((OWN, D), BF16),) * 2,
        (whole((3, rows, HID)), whole((HALF, D))) + (whole((OWN, D)),) * 2,
        1,
        "attend_back",
        cost(2 * rows * D * 5 * HID, 2 * 4 * HID * D + 8 * rows * D),
        scratch=[pltpu.VMEM((rows, D), F32)],
        after=after,
    )


def feed_kernel(width_ref, core_ref, a_ref, up_ref, down_ref, hid_ref, slope_ref, pm_ref, pt_ref, acc):
    step = pl.program_id(0)
    u = dot(a_ref[...], up_ref[0])
    place = lax.broadcasted_iota(jnp.int32, u.shape, 1) + step * FB
    keep = place < width_ref[0]
    square = u * u
    t = jnp.tanh(C1 * (u + C2 * u * square))
    hid = jnp.where(keep, 0.5 * u * (1.0 + t), 0.0).astype(BF16)
    slope = 0.5 * (1.0 + t) + 0.5 * u * (1.0 - t * t) * (C1 * (1.0 + 3.0 * C2 * square))
    slope_ref[...] = jnp.where(keep, slope, 0.0).astype(BF16)
    hid_ref[...] = hid
    part = dot(hid, down_ref[0])

    @pl.when(step == 0)
    def _():
        acc[...] = part

    @pl.when(step > 0)
    def _():
        acc[...] += part

    @pl.when(step == SLICE // FB - 1)
    def _():
        mine_theirs(core_ref[0], acc, pm_ref, (pt_ref,))


def feed(layer, width, core, a, w_up, w_down, after=()):
    piece = whole((OWN, D))
    block = pl.BlockSpec((HALF, FB), lambda j: (0, j))
    return run(
        feed_kernel,
        (width, core, a, w_up, w_down),
        [
            SMEM,
            SMEM,
            whole((HALF, D)),
            pl.BlockSpec((1, D, FB), lambda j: (layer, 0, j)),
            pl.BlockSpec((1, FB, D), lambda j: (layer, j, 0)),
        ],
        (
            jax.ShapeDtypeStruct((HALF, SLICE), BF16),
            jax.ShapeDtypeStruct((HALF, SLICE), BF16),
            jax.ShapeDtypeStruct((OWN, D), BF16),
            jax.ShapeDtypeStruct((OWN, D), BF16),
        ),
        (block, block, piece, piece),
        SLICE // FB,
        "feed",
        cost(4 * HALF * D * SLICE, 4 * SLICE * D + 8 * HALF * D),
        scratch=[pltpu.VMEM((HALF, D), F32)],
        after=after,
    )


def feed_back_kernel(core_ref, g0_ref, g1_ref, down_ref, up_ref, slope0_ref, slope1_ref, du_ref, *rest):
    outs, acc = rest[:3], rest[3]
    step = pl.program_id(0)
    g = jnp.concatenate([g0_ref[...], g1_ref[...]], axis=0)
    dhid = dot_t(g, down_ref[0])
    slope = jnp.concatenate([slope0_ref[...], slope1_ref[...]], axis=0).astype(F32)
    du = (dhid * slope).astype(BF16)
    du_ref[...] = du
    part = dot_t(du, up_ref[0])

    @pl.when(step == 0)
    def _():
        acc[...] = part

    @pl.when(step > 0)
    def _():
        acc[...] += part

    @pl.when(step == SLICE // FB - 1)
    def _():
        mine_theirs(core_ref[0], acc, outs[0], outs[1:])


def feed_back(layer, core, g0, g1, w_up, w_down, slope0, slope1, after=()):
    rows = 2 * HALF
    piece = whole((HALF, D))
    block = pl.BlockSpec((HALF, FB), lambda j: (0, j))
    return run(
        feed_back_kernel,
        (core, g0, g1, w_down, w_up, slope0, slope1),
        [
            SMEM,
            piece,
            piece,
            pl.BlockSpec((1, FB, D), lambda j: (layer, j, 0)),
            pl.BlockSpec((1, D, FB), lambda j: (layer, 0, j)),
            block,
            block,
        ],
        (
            jax.ShapeDtypeStruct((rows, SLICE), BF16),
        )
        + (jax.ShapeDtypeStruct((HALF, D), BF16),)
        + (jax.ShapeDtypeStruct((OWN, D), BF16),) * 2,
        (pl.BlockSpec((rows, FB), lambda j: (0, j)), whole((HALF, D))) + (whole((OWN, D)),) * 2,
        SLICE // FB,
        "feed_back",
        cost(4 * rows * D * SLICE, 4 * SLICE * D + 8 * rows * D),
        scratch=[pltpu.VMEM((rows, D), F32)],
        after=after,
    )


def block_at(place_ref, major, minor, d):
    there = lax.rem(place_ref[0] + d, 4)
    block = major * 16 + minor * place_ref[3] + there * place_ref[4]
    return pl.multiple_of(block * 48, 16)


RING = (
    (384, ((0, 0), (0, 1))),
    (384, ((2, 1), (1, 0))),
    (384, ((2, 0), (3, 1))),
    (192, ((1, 1),)),
    (192, ((3, 0),)),
)


def grad_kernel(terms, place_ref, *refs):
    lefts = refs[: sum(t[0] for t in terms)]
    refs = refs[len(lefts) :]
    rights = refs[: sum(t[1] for t in terms)]
    refs = refs[len(rights) :]
    outs, (turned, total) = refs[:-2], refs[-2:]
    step = pl.program_id(0)
    start = at_left = at_right = 0
    for count, operands, number in terms:
        left = lefts[at_left : at_left + count]
        right = rights[at_right : at_right + operands]
        at_left += count
        at_right += operands

        @pl.when(step == start)
        def _():
            turned[...] = jnp.concatenate([r[...] for r in left], axis=0).T

        @pl.when((step >= start) & (step < start + number))
        def _():
            b = jnp.concatenate([r[0] if len(r.shape) == 3 else r[...] for r in right], axis=0)
            total[...] = dot(turned[...], b).astype(BF16)

        start += number
    for out, (_, pieces) in zip(outs, RING):
        for n, (d, major) in enumerate(pieces):
            for minor in range(4):
                row = (n * 4 + minor) * 48
                out[row : row + 48, :] = total[pl.ds(block_at(place_ref, major, minor, d), 48), :]


def grads(place, block, terms, after=()):
    lefts, specs, rights, right_specs = [], [], [], []
    counts, start = [], 0
    for left, right, number in terms:
        lefts += left
        specs += [whole(a.shape) for a in left]
        counts.append((len(left), len(right), number))
        for array, shape, index in right:
            rights.append(array)
            right_specs.append(
                pl.BlockSpec(
                    shape,
                    lambda j, s=start, n=number, index=index: index(jnp.clip(j - s, 0, n - 1)),
                )
            )
        start += number
    columns = start * block
    return run(
        functools.partial(grad_kernel, counts),
        (place, *lefts, *rights),
        [SMEM] + specs + right_specs,
        (pltpu.HBM((384, columns), BF16),)
        + tuple(jax.ShapeDtypeStruct((n, columns), BF16) for n, _ in RING[1:]),
        tuple(pl.BlockSpec((n, block), lambda j: (0, j)) for n, _ in RING),
        start,
        "grads",
        cost(4 * HALF * D * columns, 3 * D * columns + 4 * HALF * (columns + D)),
        scratch=[pltpu.VMEM((D, 2 * HALF), BF16), pltpu.VMEM((D, block), BF16)],
        after=after,
    )


def merge_kernel(*refs):
    ins, outs = refs[:4], refs[4:]
    for number, out in enumerate(outs):
        own, got = ins[2 * number : 2 * number + 2]
        out[...] = (own[...].astype(F32) + got[...].astype(F32)).astype(BF16)


def in_two(values):
    high = values.astype(BF16).astype(F32)
    return jnp.concatenate([high, values - high], axis=0).astype(BF16)


def from_two(pairs_of_rows):
    t = pairs_of_rows.astype(F32)
    return t[:8] + t[8:]


def sum_kernel(groups, place_ref, *refs):
    rider, refs = (refs[0], refs[1:]) if len(refs) % 5 == 1 else (None, refs)
    ins, outs, total = refs[: 5 * len(groups)], refs[5 * len(groups) : -1], refs[-1]
    step = pl.program_id(0)
    for number, (begin, end) in enumerate(groups):
        own, left_a, right_b, right_a, left_b = ins[5 * number : 5 * number + 5]

        @pl.when((step >= begin) & (step < end))
        def _():
            for at, one, two in ((0, left_a, right_a), (192, right_b, left_b)):
                t = own[at : at + 192].astype(F32) + one[...].astype(F32) + two[...].astype(F32)
                total[at : at + 192] = t.astype(BF16)

    for d, out in enumerate(outs):
        there = lax.rem(place_ref[1] + d, 4)
        for major in range(2):
            offset = pl.multiple_of((major * 4 + there) * 48, 16)
            out[major * 48 : (major + 1) * 48, :] = total[pl.ds(offset, 48), :]
        if rider is not None:
            out[96:112, :] = in_two(rider[...])


def last_kernel(rides, place_ref, *refs):
    ins, (keep, away, *ridden, total) = refs[:4], refs[4:]
    here = place_ref[2]
    total[...] = sum(r[:96].astype(F32) for r in ins)
    keep[...] = total[pl.ds(pl.multiple_of(here * 48, 16), 48), :]
    away[...] = total[pl.ds(pl.multiple_of((1 - here) * 48, 16), 48), :].astype(BF16)
    if rides:
        a, b, c, d = (from_two(r[96:112]) for r in ins)

        @pl.when(pl.program_id(0) == 0)
        def _():
            ridden[0][...] = (a + c) + (b + d)


def add_kernel(a_ref, b_ref, o_ref):
    o_ref[...] = a_ref[...] + b_ref[...].astype(F32)


def add_small(a, b, after):
    spec = whole(a.shape)
    return run(
        add_kernel,
        [a, b],
        [spec] * 2,
        jax.ShapeDtypeStruct(a.shape, F32),
        spec,
        1,
        "add",
        cost(a.size, 12 * a.size),
        after=after,
    )


class Ring:
    def __init__(self, parts):
        self.own, right, left, *self.later = parts
        self.from_left = send(right, ring_by(False, 1))
        self.from_right = send(left, ring_by(False, 3))
        self.columns = self.own.shape[1]

    def merge(self, after=()):
        block = 768
        spec = pl.BlockSpec((192, block), lambda j: (0, j))
        right, left = outs = run(
            merge_kernel,
            [self.later[0], self.from_left, self.later[1], self.from_right],
            [spec] * 4,
            (jax.ShapeDtypeStruct((192, self.columns), BF16),) * 2,
            (spec,) * 2,
            self.columns // block,
            "merge",
            cost(2 * 192 * self.columns, 12 * 192 * self.columns),
            after=after,
        )
        self.left_b = send(right, ring_by(False, 1))
        self.right_a = send(left, ring_by(False, 3))
        return (right,)


class Finish:
    def __init__(self, place, rings, after=(), rider=None):
        self.place = place
        self.rides = rider is not None
        block = 768
        args, specs, groups, begin = [], [], [], 0
        if self.rides:
            args.append(rider)
            specs.append(pl.BlockSpec((8, block), lambda j: (0, jnp.minimum(j, 1))))
        for r in rings:
            number = r.columns // block

            def spec(rows, half, s=begin, n=number):
                return pl.BlockSpec((rows, block), lambda j: (half, jnp.clip(j - s, 0, n - 1)))

            args += [far(r.own), r.from_left, r.from_right, r.right_a, r.left_b]
            specs += [spec(384, 0), spec(192, 1), spec(192, 1), spec(192, 0), spec(192, 0)]
            groups.append((begin, begin + number))
            begin += number
        self.columns = begin * block
        self.rows = 112 if self.rides else 96
        outs = run(
            functools.partial(sum_kernel, groups),
            [place] + args,
            [SMEM] + specs,
            (jax.ShapeDtypeStruct((self.rows, self.columns), BF16),) * 4,
            (pl.BlockSpec((self.rows, block), lambda j: (0, j)),) * 4,
            begin,
            "sum_rings",
            cost(3 * 384 * self.columns, 8 * 384 * self.columns),
            scratch=[pltpu.VMEM((384, block), BF16)],
            after=after,
        )
        self.got = [outs[0]] + [send(outs[d], ring_by(True, d)) for d in (1, 2, 3)]
        self.gate = outs[:1]

    def last(self, after=()):
        block = 1536
        spec = pl.BlockSpec((self.rows, block), lambda j: (0, j))
        riding = (jax.ShapeDtypeStruct((8, D), F32),) if self.rides else ()
        self.keep, away, *ridden = run(
            functools.partial(last_kernel, self.rides),
            [self.place, *self.got],
            [SMEM] + [spec] * 4,
            (
                jax.ShapeDtypeStruct((48, self.columns), F32),
                jax.ShapeDtypeStruct((48, self.columns), BF16),
            )
            + riding,
            (
                pl.BlockSpec((48, block), lambda j: (0, j)),
                pl.BlockSpec((48, block), lambda j: (0, j)),
            )
            + (whole((8, D)),) * len(riding),
            self.columns // block,
            "sum_last",
            cost(4 * 96 * self.columns, 12 * 96 * self.columns),
            scratch=[pltpu.VMEM((96, block), F32)],
            after=after,
        )
        self.arrived = send(away, ZLO)
        if self.rides:
            self.ridden = ridden[0]
        return (away,)


def finish_kernel(*refs):
    ins, (up, down, qkv, out) = refs[:4], refs[4:]
    for layer in range(2):
        keep, arrived = ins[2 * layer : 2 * layer + 2]
        total = keep[...] + arrived[...].astype(F32)
        up[layer] = total[:, :SLICE]
        down[layer] = total[:, SLICE : 2 * SLICE]
        for n in range(3):
            qkv[layer, n] = total[:, 2 * SLICE + n * HID : 2 * SLICE + (n + 1) * HID]
        out[layer] = total[:, 2 * SLICE + 3 * HID :]


def finish(layers):
    shapes = [(2, 48, SLICE), (2, 48, SLICE), (2, 3, 48, HID), (2, 48, HID)]
    columns = layers[0].columns
    return run(
        finish_kernel,
        [a for layer in layers for a in (layer.keep, layer.arrived)],
        [whole((48, columns))] * 4,
        tuple(jax.ShapeDtypeStruct(shape, F32) for shape in shapes),
        tuple(whole(shape) for shape in shapes),
        1,
        "finish",
        cost(96 * columns, 20 * 48 * columns),
    )


def body(tokens, norm_gain, norm_shift, w_qkv, w_out, w_up, w_down, granularity, cotangent):
    zl, y, x, zh, c = (lax.axis_index(a) for a in AXES)
    layers = w_qkv.shape[0]
    core = c.reshape(1).astype(jnp.int32)
    place = jnp.where(c == 0, jnp.stack([x, y, zl, 4, 1]), jnp.stack([y, x, zl, 1, 4]))
    place = place.astype(jnp.int32)
    width = FF // 8 * 2 ** granularity[0, 0] - (zh * 2 + c) * SLICE
    width = width.reshape(1).astype(jnp.int32)
    w_qkv = jnp.transpose(w_qkv, (0, 2, 1, 3))
    low_chip = zh == 0

    positions = jnp.arange(2 * HALF, dtype=F32)[:, None]
    half = E // 2
    frequency = BASE ** (-jnp.arange(half, dtype=F32) / half)
    angles = positions * frequency[None, :]
    cos = jnp.cos(angles)
    sin = jnp.sin(angles)
    cos = jnp.concatenate([cos, cos], axis=1)
    sin = jnp.concatenate([-sin, sin], axis=1)

    def gain(layer, member):
        return norm_gain[layer, member][None, :]

    def shift(layer, member):
        return norm_shift[layer, member][None, :]

    def both_chunks(own):
        other = send(own, FAR)
        return jnp.where(low_chip, own, other), jnp.where(low_chip, other, own)

    def pair(a):
        return lax.all_gather(a, "c", axis=0, tiled=True)

    def core_sum(mine, *theirs):
        other = [lax.dynamic_slice_in_dim(pair(t), (1 - c) * OWN, OWN, 0) for t in theirs]
        return mine.astype(F32) + jnp.concatenate(other, axis=0).astype(F32)

    def exchange(mine, *theirs):
        s = core_sum(mine, *theirs).astype(BF16)
        return s, send(s, FAR)

    stream = list(both_chunks(tokens))
    normed = [pair(norm(stream[k], gain(0, 0), shift(0, 0))) for k in range(2)]
    saved = []
    gate = ()
    sums = [None] * 2
    for layer in range(layers):
        last = layer == layers - 1
        qkv, mixture, hid, slope = ([None] * 2 for _ in range(4))
        mid, normed_two, following = ([None] * 2 for _ in range(3))
        if layer:
            normed = [None] * 2
        for k in range(2):
            if layer:
                stream[k], a = add_norm(mid_before[k], *sums[k], gain(layer, 0), shift(layer, 0), gate)
                normed[k] = pair(a)
            qkv[k], mixture[k], pm, pt = attend(
                layer, k, core, normed[k], w_qkv, w_out, cos, sin, qkv[0], gate
            )
            sums[k] = exchange(pm, pt)
            gate = sums[k][:1]
        keep = {"stream": list(stream), "normed": normed}
        for k in range(2):
            mid[k], a = add_norm(stream[k], *sums[k], gain(layer, 1), shift(layer, 1), gate)
            normed_two[k] = pair(a)
            hid[k], slope[k], pm, pt = feed(layer, width, core, normed_two[k], w_up, w_down, gate)
            if last:
                sums[k] = core_sum(pm, pt)
                gate = (pm,)
            else:
                sums[k] = exchange(pm, pt)
                gate = sums[k][:1]
        mid_before = mid
        keep.update(qkv=qkv, mixture=mixture, mid=mid, normed_two=normed_two, hid=hid, slope=slope)
        saved.append(keep)
    ours = jnp.where(low_chip, sums[0], sums[1])
    away = jnp.where(low_chip, sums[1], sums[0]).astype(BF16)
    base = jnp.where(low_chip, mid[0], mid[1])
    came = send(away, FAR)
    activations = (base + (ours + came.astype(F32))).astype(BF16)

    gradient = both_chunks(cotangent)
    g = [pair(v) for v in gradient]
    norm_sums = [[None, None] for _ in range(layers)]

    def column(j):
        return (0, j)

    def feed_grads(kept, du, g, after):
        number = SLICE // FB
        parts = grads(
            place,
            FB,
            [
                ([far(a) for a in kept["normed_two"]], [(du, (2 * HALF, FB), column)], number),
                (g, [(far(h), (HALF, FB), column) for h in kept["hid"]], number),
            ],
            after,
        )
        return Ring(parts), parts[4:]

    def attend_grads(kept, dqkv, g, after):
        head = (1, 2 * HALF, HID)
        parts = grads(
            place,
            HID,
            [
                ([far(a) for a in kept["normed"]], [(dqkv, head, lambda j: (j, 0, 0))], 3),
                (g, [(far(m), (HALF, HID), lambda j: (0, 0)) for m in kept["mixture"]], 1),
            ],
            after,
        )
        return Ring(parts), parts[4:]

    one, zero = layers - 1, 0
    kept = saved[one]
    du, *parts = feed_back(one, core, *g, w_up, w_down, *kept["slope"], gate)
    s, r = exchange(*parts)
    feed_one, gate = feed_grads(kept, du, g, (s,))
    gradient, low, norm_sums[one][1] = norm_back(kept["mid"], s, r, gradient, gain(one, 1), gate)
    g = [pair(v) for v in low]
    dqkv, *parts = attend_back(one, core, *g, w_qkv, w_out, cos, sin, *kept["qkv"])
    s, r = exchange(*parts)
    gate = feed_one.merge((s,))
    attend_one, gate = attend_grads(kept, dqkv, g, gate)
    gradient, low, norm_sums[one][0] = norm_back(
        kept["stream"], s, r, gradient, gain(one, 0), gate
    )
    g = [pair(v) for v in low]
    kept = saved[zero]
    early = (attend_one.from_left, attend_one.from_right)
    du, *parts = feed_back(zero, core, *g, w_up, w_down, *kept["slope"], early)
    s, r = exchange(*parts)
    gate = attend_one.merge((s,))
    feed_zero, gate = feed_grads(kept, du, g, gate)
    layer_one = Finish(place, [feed_one, attend_one], gate)
    gate = layer_one.gate
    gradient, low, norm_sums[zero][1] = norm_back(
        kept["mid"], s, r, gradient, gain(zero, 1), gate
    )
    g = [pair(v) for v in low]
    dqkv, *parts = attend_back(zero, core, *g, w_qkv, w_out, cos, sin, *kept["qkv"])
    total = core_sum(*parts)
    s = jnp.where(low_chip, total[:OWN], total[OWN:]).astype(BF16)
    away = jnp.where(low_chip, total[OWN:], total[:OWN]).astype(BF16)
    r = send(away, FAR)
    attend_zero, gate = attend_grads(kept, dqkv, g, (away,))
    gate = feed_zero.merge(gate)
    gate = layer_one.last(gate)
    xs = jnp.where(low_chip, *kept["stream"])
    prev = jnp.where(low_chip, *gradient)
    (input_grad,), _, norm_sums[zero][0] = norm_back([xs], s, r, [prev], gain(zero, 0), gate)
    gate = attend_zero.merge((input_grad,))
    half = [0.5 * norm_sums[zero][1], 0.5 * norm_sums[one][0], 0.5 * norm_sums[one][1]]
    sums = jnp.concatenate([norm_sums[zero][0], *half], axis=0)
    sums = sums + send(sums, FAR)
    layer_zero = Finish(place, [feed_zero, attend_zero], (*gate, layer_one.arrived), sums)
    layer_zero.last((came,))
    sums = layer_zero.ridden
    grad_up, grad_down, grad_qkv, grad_out = finish([layer_zero, layer_one])
    one_on, two_on, three_on = (send(sums, ring_by(False, d)) for d in (1, 2, 3))
    sums = (sums + two_on) + (one_on + three_on)
    sums = add_small(sums, send(sums, ZLO), (grad_up,))
    sums = jnp.sum(lax.all_gather(sums, "c", axis=0), axis=0)
    sums = sums.reshape(layers, 2, 2, D)
    gain_grads, shift_grads = sums[:, :, 0], sums[:, :, 1]

    grad_qkv = jnp.transpose(grad_qkv, (0, 2, 1, 3))
    grad_down = jnp.swapaxes(grad_down, 1, 2)
    grad_out = jnp.swapaxes(grad_out, 1, 2)
    return (
        activations,
        input_grad,
        grad_qkv,
        grad_out,
        grad_up,
        grad_down,
        gain_grads,
        shift_grads,
        shift_grads[:, 1, :],
    )


def solution(mesh):
    fine = Mesh(mesh.devices.reshape(SIZES), AXES)
    rows = P(AXES, None)
    dp, tensor = AXES[:3], AXES[3:]
    return jax.shard_map(
        body,
        mesh=fine,
        in_specs=(
            rows,
            P(),
            P(),
            P(None, None, None, tensor),
            P(None, tensor, None),
            P(None, None, tensor),
            P(None, tensor, None),
            P(dp, None),
            rows,
        ),
        out_specs=(
            rows,
            rows,
            P(None, dp, None, tensor),
            P(None, tensor, dp),
            P(None, dp, tensor),
            P(None, tensor, dp),
            P(),
            P(),
            P(),
        ),
        check_vma=False,
    )
```

```python
import functools
import itertools

import jax
import jax.numpy as jnp
from jax import lax
from jax.experimental import pallas as pl
from jax.experimental.pallas import tpu as pltpu
from jax.sharding import Mesh
from jax.sharding import PartitionSpec as P

D = 1536
FF = 6144
E = 128
HEADS = 3
HID = HEADS * E
SLICE = 1536
HALF = 256
OWN = 128
FB = 512
EPS = 1e-5
BASE = 10000.0
MASKED = -1e30
SCALE = E**-0.5
C1 = 0.7978845608028654
C2 = 0.044715

AXES = ("zl", "y", "x", "zh", "c")
SIZES = (2, 4, 4, 2, 2)
F32 = jnp.float32
BF16 = jnp.bfloat16


def flat(place):
    index = 0
    for size, at in zip(SIZES, place):
        index = index * size + at
    return index


def pairs(move):
    return [
        (flat(p), flat(move(*p))) for p in itertools.product(*[range(s) for s in SIZES])
    ]


FAR = pairs(lambda zl, y, x, zh, c: (zl, y, x, 1 - zh, c))
ZLO = pairs(lambda zl, y, x, zh, c: (1 - zl, y, x, zh, c))


def ring_by(second, d):
    def move(zl, y, x, zh, c):
        if (c == 0) != second:
            return zl, y, (x + d) % 4, zh, c
        return zl, (y + d) % 4, x, zh, c

    return pairs(move)


def send(values, perm):
    return lax.ppermute(values, AXES, perm)


def dot(a, b):
    return jnp.dot(a, b, preferred_element_type=F32)


def dot_t(a, b):
    return lax.dot_general(a, b, (((1,), (1,)), ((), ())), preferred_element_type=F32)


def t_dot(a, b):
    return lax.dot_general(a, b, (((0,), (0,)), ((), ())), preferred_element_type=F32)


VMEM_MB = {
    "attend": 18,
    "attend_back": 28,
    "feed": 16,
    "feed_back": 21,
    "grads": 20,
    "merge": 12,
    "sum_rings": 12,
    "sum_last": 12,
    "finish": 12,
    "norm": 8,
    "add": 8,
    "add_norm": 8,
    "norm_back": 14,
}


def params(mb):
    return pltpu.CompilerParams(vmem_limit_bytes=mb * 1024 * 1024)


def cost(flops, size, trans=0):
    return pl.CostEstimate(flops=1, bytes_accessed=1, transcendentals=0)


def whole(shape):
    zeros = (0,) * len(shape)
    return pl.BlockSpec(shape, lambda *_: zeros)


SMEM = pl.BlockSpec(memory_space=pltpu.SMEM)
ANY = pl.BlockSpec(memory_space=pl.ANY)


def far(a):
    return pltpu.with_memory_space_constraint(a, pltpu.HBM)


def run(kernel, args, in_specs, out_shape, out_specs, grid, name, estimate, scratch=(), after=()):
    count, extra = len(args), len(after)

    def wrapped(*refs):
        kernel(*refs[:count], *refs[count + extra :])

    return pl.pallas_call(
        wrapped,
        out_shape=out_shape,
        in_specs=list(in_specs) + [ANY] * extra,
        out_specs=out_specs,
        scratch_shapes=list(scratch),
        grid=(grid,),
        compiler_params=params(VMEM_MB[name]),
        cost_estimate=estimate,
        name=name,
    )(*args, *after)


def moments(x):
    mean = jnp.mean(x, axis=-1, keepdims=True)
    centered = x - mean
    var = jnp.mean(centered * centered, axis=-1, keepdims=True)
    return centered, lax.rsqrt(var + EPS)


def norm_kernel(x_ref, g_ref, b_ref, a_ref):
    centered, r = moments(x_ref[...].astype(F32))
    a_ref[...] = (centered * r * g_ref[...] + b_ref[...]).astype(BF16)


def norm(x, gain, shift):
    rows = x.shape[0]
    return run(
        norm_kernel,
        (x, gain, shift),
        [whole((rows, D)), whole((1, D)), whole((1, D))],
        jax.ShapeDtypeStruct((rows, D), BF16),
        whole((rows, D)),
        1,
        "norm",
        cost(10 * rows * D, 6 * rows * D),
    )


def add_norm_kernel(x_ref, s_ref, r_ref, g_ref, b_ref, m_ref, a_ref):
    x = x_ref[...].astype(F32) + (s_ref[...].astype(F32) + r_ref[...].astype(F32))
    m_ref[...] = x
    centered, r = moments(x)
    a_ref[...] = (centered * r * g_ref[...] + b_ref[...]).astype(BF16)


def add_norm(x, s, r, gain, shift, after=()):
    rows = x.shape[0]
    return run(
        add_norm_kernel,
        (x, s, r, gain, shift),
        [whole((rows, D))] * 3 + [whole((1, D))] * 2,
        (jax.ShapeDtypeStruct((rows, D), F32), jax.ShapeDtypeStruct((rows, D), BF16)),
        (whole((rows, D)), whole((rows, D))),
        1,
        "add_norm",
        cost(10 * rows * D, 14 * rows * D),
        after=after,
    )


def norm_back_kernel(count, *refs):
    xs, prevs = refs[:count], refs[count : 2 * count]
    s_ref, r_ref, g_ref = refs[2 * count : 2 * count + 3]
    refs = refs[2 * count + 3 :]
    ds, lows, sums_ref = refs[:count], refs[count : 2 * count], refs[2 * count]
    for k in range(count):
        rows = slice(k * OWN, (k + 1) * OWN)
        da = s_ref[rows, :].astype(F32) + r_ref[rows, :].astype(F32)
        centered, r = moments(xs[k][...].astype(F32))
        xh = centered * r
        e = da * g_ref[...]
        mean_e = jnp.mean(e, axis=-1, keepdims=True)
        mean_ex = jnp.mean(e * xh, axis=-1, keepdims=True)
        out = prevs[k][...].astype(F32) + r * (e - mean_e - xh * mean_ex)
        ds[k][...] = out
        lows[k][...] = out.astype(BF16)
        both = (jnp.sum(da * xh, axis=0, keepdims=True), jnp.sum(da, axis=0, keepdims=True))
        for n in range(2):
            if k:
                sums_ref[n : n + 1, :] += both[n]
            else:
                sums_ref[n : n + 1, :] = both[n]


def norm_back(xs, s, r, prevs, gain, after=()):
    count = len(xs)
    piece = whole((OWN, D))
    outs = run(
        functools.partial(norm_back_kernel, count),
        (*xs, *prevs, s, r, gain),
        [piece] * (2 * count) + [whole((count * OWN, D))] * 2 + [whole((1, D))],
        (jax.ShapeDtypeStruct((OWN, D), F32),) * count
        + (jax.ShapeDtypeStruct((OWN, D), BF16),) * count
        + (jax.ShapeDtypeStruct((2, D), F32),),
        (piece,) * (2 * count) + (whole((2, D)),),
        1,
        "norm_back",
        cost(20 * count * OWN * D, 18 * count * OWN * D),
        after=after,
    )
    return outs[:count], outs[count : 2 * count], outs[2 * count]


def rot(x, cos, sin):
    return x * cos + pltpu.roll(x, E // 2, 1) * sin


def allowed(q_start, rows, columns):
    q = lax.broadcasted_iota(jnp.int32, (rows, columns), 0) + q_start
    return lax.broadcasted_iota(jnp.int32, (rows, columns), 1) <= q


def mine_theirs(core, acc, mine, theirs):
    for k, out in enumerate(theirs):
        here, there = (
            pl.ds(pl.multiple_of(k * HALF + side * OWN, OWN), OWN) for side in (core, 1 - core)
        )
        mine[k * OWN : (k + 1) * OWN, :] = acc[here, :].astype(BF16)
        out[...] = acc[there, :].astype(BF16)


def softmax(s):
    top = jnp.max(s, axis=-1, keepdims=True)
    e = jnp.exp(s - top)
    return e * (1.0 / jnp.sum(e, axis=-1, keepdims=True))


def attend_kernel(chunk, core_ref, a_ref, w_ref, wo_ref, cos_ref, sin_ref, *rest):
    if chunk:
        before_ref, qkv_ref, o_ref, pm_ref, pt_ref, acc = rest
    else:
        qkv_ref, o_ref, pm_ref, pt_ref, acc = rest
    a = a_ref[...]
    cos, sin = cos_ref[...], sin_ref[...]
    pq, pk, pv = (dot(a, w_ref[0, n]) for n in range(3))
    mask = allowed(chunk * HALF, HALF, HALF * (chunk + 1))
    for h in range(HEADS):
        cols = slice(h * E, (h + 1) * E)
        q = (rot(pq[:, cols], cos, sin) * SCALE).astype(BF16)
        k = rot(pk[:, cols], cos, sin).astype(BF16)
        v = pv[:, cols].astype(BF16)
        qkv_ref[0, :, cols], qkv_ref[1, :, cols], qkv_ref[2, :, cols] = q, k, v
        if chunk:
            k = jnp.concatenate([before_ref[1, :, cols], k], axis=0)
            v = jnp.concatenate([before_ref[2, :, cols], v], axis=0)
        s = jnp.where(mask, dot_t(q, k), MASKED)
        o_ref[:, cols] = dot(softmax(s).astype(BF16), v).astype(BF16)
    acc[...] = dot(o_ref[...], wo_ref[0])
    mine_theirs(core_ref[0], acc, pm_ref, (pt_ref,))


def attend(layer, chunk, core, a, w_qkv, w_out, cos, sin, before, after=()):
    head = whole((3, HALF, HID))
    tables = pl.BlockSpec((HALF, E), lambda h: (chunk, 0))
    piece = whole((OWN, D))
    return run(
        functools.partial(attend_kernel, chunk),
        (core, a, w_qkv, w_out, cos, sin) + ((before,) if chunk else ()),
        [
            SMEM,
            whole((HALF, D)),
            pl.BlockSpec((1, 3, D, HID), lambda h: (layer, 0, 0, 0)),
            pl.BlockSpec((1, HID, D), lambda h: (layer, 0, 0)),
            tables,
            tables,
        ]
        + ([head] if chunk else []),
        (
            jax.ShapeDtypeStruct((3, HALF, HID), BF16),
            jax.ShapeDtypeStruct((HALF, HID), BF16),
            jax.ShapeDtypeStruct((OWN, D), BF16),
            jax.ShapeDtypeStruct((OWN, D), BF16),
        ),
        (head, whole((HALF, HID)), piece, piece),
        1,
        "attend",
        cost(2 * HALF * D * 4 * HID, 2 * 4 * HID * D + 8 * HALF * D),
        scratch=[pltpu.VMEM((HALF, D), F32)],
        after=after,
    )


def attend_back_kernel(
    core_ref, g0_ref, g1_ref, w_ref, wo_ref, cos_ref, sin_ref, c0_ref, c1_ref, d_ref, *rest
):
    outs, acc = rest[:3], rest[3]
    do0 = dot_t(g0_ref[...], wo_ref[0]).astype(BF16)
    do1 = dot_t(g1_ref[...], wo_ref[0]).astype(BF16)
    cos, sin = cos_ref[...], -sin_ref[...]
    masks = [allowed(n * HALF, HALF, HALF * (n + 1)) for n in range(2)]

    def block(chunk, q, do, keys, values):
        prob = softmax(jnp.where(masks[chunk], dot_t(q, keys), MASKED))
        dp = dot_t(do, values)
        ds = (prob * (dp - jnp.sum(prob * dp, axis=-1, keepdims=True))).astype(BF16)
        return dot(ds, keys), t_dot(ds, q), t_dot(prob.astype(BF16), do)

    for h in range(HEADS):
        cols = slice(h * E, (h + 1) * E)
        q0, k0, v0 = (c0_ref[n, :, cols] for n in range(3))
        q1, k1, v1 = (c1_ref[n, :, cols] for n in range(3))
        k = jnp.concatenate([k0, k1], axis=0)
        v = jnp.concatenate([v0, v1], axis=0)
        dq1, dk1, dv1 = block(1, q1, do1[:, cols], k, v)
        dq0, dk0, dv0 = block(0, q0, do0[:, cols], k0, v0)
        dq = rot(jnp.concatenate([dq0, dq1], axis=0), cos, sin) * SCALE
        dk = rot(jnp.concatenate([dk0 + dk1[:HALF], dk1[HALF:]], axis=0), cos, sin)
        dv = jnp.concatenate([dv0 + dv1[:HALF], dv1[HALF:]], axis=0)
        for n, value in enumerate((dq, dk, dv)):
            d_ref[n, :, cols] = value.astype(BF16)
    acc[...] = sum(dot_t(d_ref[n], w_ref[0, n]) for n in range(3))
    mine_theirs(core_ref[0], acc, outs[0], outs[1:])


def attend_back(layer, core, g0, g1, w_qkv, w_out, cos, sin, saved0, saved1, after=()):
    rows = 2 * HALF
    head = whole((3, HALF, HID))
    piece = whole((HALF, D))
    return run(
        attend_back_kernel,
        (core, g0, g1, w_qkv, w_out, cos, sin, saved0, saved1),
        [
            SMEM,
            piece,
            piece,
            pl.BlockSpec((1, 3, D, HID), lambda h: (layer, 0, 0, 0)),
            pl.BlockSpec((1, HID, D), lambda h: (layer, 0, 0)),
            whole((rows, E)),
            whole((rows, E)),
            head,
            head,
        ],
        (
            jax.ShapeDtypeStruct((3, rows, HID), BF16),
        )
        + (jax.ShapeDtypeStruct((HALF, D), BF16),)
        + (jax.ShapeDtypeStruct((OWN, D), BF16),) * 2,
        (whole((3, rows, HID)), whole((HALF, D))) + (whole((OWN, D)),) * 2,
        1,
        "attend_back",
        cost(2 * rows * D * 5 * HID, 2 * 4 * HID * D + 8 * rows * D),
        scratch=[pltpu.VMEM((rows, D), F32)],
        after=after,
    )


def feed_kernel(width_ref, core_ref, a_ref, up_ref, down_ref, hid_ref, slope_ref, pm_ref, pt_ref, acc):
    step = pl.program_id(0)
    u = dot(a_ref[...], up_ref[0])
    place = lax.broadcasted_iota(jnp.int32, u.shape, 1) + step * FB
    keep = place < width_ref[0]
    square = u * u
    t = jnp.tanh(C1 * (u + C2 * u * square))
    hid = jnp.where(keep, 0.5 * u * (1.0 + t), 0.0).astype(BF16)
    slope = 0.5 * (1.0 + t) + 0.5 * u * (1.0 - t * t) * (C1 * (1.0 + 3.0 * C2 * square))
    slope_ref[...] = jnp.where(keep, slope, 0.0).astype(BF16)
    hid_ref[...] = hid
    part = dot(hid, down_ref[0])

    @pl.when(step == 0)
    def _():
        acc[...] = part

    @pl.when(step > 0)
    def _():
        acc[...] += part

    @pl.when(step == SLICE // FB - 1)
    def _():
        mine_theirs(core_ref[0], acc, pm_ref, (pt_ref,))


def feed(layer, width, core, a, w_up, w_down, after=()):
    piece = whole((OWN, D))
    block = pl.BlockSpec((HALF, FB), lambda j: (0, j))
    return run(
        feed_kernel,
        (width, core, a, w_up, w_down),
        [
            SMEM,
            SMEM,
            whole((HALF, D)),
            pl.BlockSpec((1, D, FB), lambda j: (layer, 0, j)),
            pl.BlockSpec((1, FB, D), lambda j: (layer, j, 0)),
        ],
        (
            jax.ShapeDtypeStruct((HALF, SLICE), BF16),
            jax.ShapeDtypeStruct((HALF, SLICE), BF16),
            jax.ShapeDtypeStruct((OWN, D), BF16),
            jax.ShapeDtypeStruct((OWN, D), BF16),
        ),
        (block, block, piece, piece),
        SLICE // FB,
        "feed",
        cost(4 * HALF * D * SLICE, 4 * SLICE * D + 8 * HALF * D),
        scratch=[pltpu.VMEM((HALF, D), F32)],
        after=after,
    )


def feed_back_kernel(core_ref, g0_ref, g1_ref, down_ref, up_ref, slope0_ref, slope1_ref, du_ref, *rest):
    outs, acc = rest[:3], rest[3]
    step = pl.program_id(0)
    g = jnp.concatenate([g0_ref[...], g1_ref[...]], axis=0)
    dhid = dot_t(g, down_ref[0])
    slope = jnp.concatenate([slope0_ref[...], slope1_ref[...]], axis=0).astype(F32)
    du = (dhid * slope).astype(BF16)
    du_ref[...] = du
    part = dot_t(du, up_ref[0])

    @pl.when(step == 0)
    def _():
        acc[...] = part

    @pl.when(step > 0)
    def _():
        acc[...] += part

    @pl.when(step == SLICE // FB - 1)
    def _():
        mine_theirs(core_ref[0], acc, outs[0], outs[1:])


def feed_back(layer, core, g0, g1, w_up, w_down, slope0, slope1, after=()):
    rows = 2 * HALF
    piece = whole((HALF, D))
    block = pl.BlockSpec((HALF, FB), lambda j: (0, j))
    return run(
        feed_back_kernel,
        (core, g0, g1, w_down, w_up, slope0, slope1),
        [
            SMEM,
            piece,
            piece,
            pl.BlockSpec((1, FB, D), lambda j: (layer, j, 0)),
            pl.BlockSpec((1, D, FB), lambda j: (layer, 0, j)),
            block,
            block,
        ],
        (
            jax.ShapeDtypeStruct((rows, SLICE), BF16),
        )
        + (jax.ShapeDtypeStruct((HALF, D), BF16),)
        + (jax.ShapeDtypeStruct((OWN, D), BF16),) * 2,
        (pl.BlockSpec((rows, FB), lambda j: (0, j)), whole((HALF, D))) + (whole((OWN, D)),) * 2,
        SLICE // FB,
        "feed_back",
        cost(4 * rows * D * SLICE, 4 * SLICE * D + 8 * rows * D),
        scratch=[pltpu.VMEM((rows, D), F32)],
        after=after,
    )


def block_at(place_ref, major, minor, d):
    there = lax.rem(place_ref[0] + d, 4)
    block = major * 16 + minor * place_ref[3] + there * place_ref[4]
    return pl.multiple_of(block * 48, 16)


RING = (
    (384, ((0, 0), (0, 1))),
    (384, ((2, 1), (1, 0))),
    (384, ((2, 0), (3, 1))),
    (192, ((1, 1),)),
    (192, ((3, 0),)),
)


def grad_kernel(terms, place_ref, *refs):
    lefts = refs[: sum(t[0] for t in terms)]
    refs = refs[len(lefts) :]
    rights = refs[: sum(t[1] for t in terms)]
    refs = refs[len(rights) :]
    outs, (turned, total) = refs[:-2], refs[-2:]
    step = pl.program_id(0)
    start = at_left = at_right = 0
    for count, operands, number in terms:
        left = lefts[at_left : at_left + count]
        right = rights[at_right : at_right + operands]
        at_left += count
        at_right += operands

        @pl.when(step == start)
        def _():
            turned[...] = jnp.concatenate([r[...] for r in left], axis=0).T

        @pl.when((step >= start) & (step < start + number))
        def _():
            b = jnp.concatenate([r[0] if len(r.shape) == 3 else r[...] for r in right], axis=0)
            total[...] = dot(turned[...], b).astype(BF16)

        start += number
    for out, (_, pieces) in zip(outs, RING):
        for n, (d, major) in enumerate(pieces):
            for minor in range(4):
                row = (n * 4 + minor) * 48
                out[row : row + 48, :] = total[pl.ds(block_at(place_ref, major, minor, d), 48), :]


def grads(place, block, terms, after=()):
    lefts, specs, rights, right_specs = [], [], [], []
    counts, start = [], 0
    for left, right, number in terms:
        lefts += left
        specs += [whole(a.shape) for a in left]
        counts.append((len(left), len(right), number))
        for array, shape, index in right:
            rights.append(array)
            right_specs.append(
                pl.BlockSpec(
                    shape,
                    lambda j, s=start, n=number, index=index: index(jnp.clip(j - s, 0, n - 1)),
                )
            )
        start += number
    columns = start * block
    return run(
        functools.partial(grad_kernel, counts),
        (place, *lefts, *rights),
        [SMEM] + specs + right_specs,
        (pltpu.HBM((384, columns), BF16),)
        + tuple(jax.ShapeDtypeStruct((n, columns), BF16) for n, _ in RING[1:]),
        tuple(pl.BlockSpec((n, block), lambda j: (0, j)) for n, _ in RING),
        start,
        "grads",
        cost(4 * HALF * D * columns, 3 * D * columns + 4 * HALF * (columns + D)),
        scratch=[pltpu.VMEM((D, 2 * HALF), BF16), pltpu.VMEM((D, block), BF16)],
        after=after,
    )


def merge_kernel(*refs):
    ins, outs = refs[:4], refs[4:]
    for number, out in enumerate(outs):
        own, got = ins[2 * number : 2 * number + 2]
        out[...] = (own[...].astype(F32) + got[...].astype(F32)).astype(BF16)


def in_two(values):
    high = values.astype(BF16).astype(F32)
    return jnp.concatenate([high, values - high], axis=0).astype(BF16)


def from_two(pairs_of_rows):
    t = pairs_of_rows.astype(F32)
    return t[:8] + t[8:]


def sum_kernel(groups, place_ref, *refs):
    rider, refs = (refs[0], refs[1:]) if len(refs) % 5 == 1 else (None, refs)
    ins, outs, total = refs[: 5 * len(groups)], refs[5 * len(groups) : -1], refs[-1]
    step = pl.program_id(0)
    for number, (begin, end) in enumerate(groups):
        own, left_a, right_b, right_a, left_b = ins[5 * number : 5 * number + 5]

        @pl.when((step >= begin) & (step < end))
        def _():
            for at, one, two in ((0, left_a, right_a), (192, right_b, left_b)):
                t = own[at : at + 192].astype(F32) + one[...].astype(F32) + two[...].astype(F32)
                total[at : at + 192] = t.astype(BF16)

    for d, out in enumerate(outs):
        there = lax.rem(place_ref[1] + d, 4)
        for major in range(2):
            offset = pl.multiple_of((major * 4 + there) * 48, 16)
            out[major * 48 : (major + 1) * 48, :] = total[pl.ds(offset, 48), :]
        if rider is not None:
            out[96:112, :] = in_two(rider[...])


def last_kernel(rides, place_ref, *refs):
    ins, (keep, away, *ridden, total) = refs[:4], refs[4:]
    here = place_ref[2]
    total[...] = sum(r[:96].astype(F32) for r in ins)
    keep[...] = total[pl.ds(pl.multiple_of(here * 48, 16), 48), :]
    away[...] = total[pl.ds(pl.multiple_of((1 - here) * 48, 16), 48), :].astype(BF16)
    if rides:
        a, b, c, d = (from_two(r[96:112]) for r in ins)

        @pl.when(pl.program_id(0) == 0)
        def _():
            ridden[0][...] = (a + c) + (b + d)


def add_kernel(a_ref, b_ref, o_ref):
    o_ref[...] = a_ref[...] + b_ref[...].astype(F32)


def add_small(a, b, after):
    spec = whole(a.shape)
    return run(
        add_kernel,
        [a, b],
        [spec] * 2,
        jax.ShapeDtypeStruct(a.shape, F32),
        spec,
        1,
        "add",
        cost(a.size, 12 * a.size),
        after=after,
    )


class Ring:
    def __init__(self, parts):
        self.own, right, left, *self.later = parts
        self.from_left = send(right, ring_by(False, 1))
        self.from_right = send(left, ring_by(False, 3))
        self.columns = self.own.shape[1]

    def merge(self, after=()):
        block = 768
        spec = pl.BlockSpec((192, block), lambda j: (0, j))
        right, left = outs = run(
            merge_kernel,
            [self.later[0], self.from_left, self.later[1], self.from_right],
            [spec] * 4,
            (jax.ShapeDtypeStruct((192, self.columns), BF16),) * 2,
            (spec,) * 2,
            self.columns // block,
            "merge",
            cost(2 * 192 * self.columns, 12 * 192 * self.columns),
            after=after,
        )
        self.left_b = send(right, ring_by(False, 1))
        self.right_a = send(left, ring_by(False, 3))
        return (right,)


class Finish:
    def __init__(self, place, rings, after=(), rider=None):
        self.place = place
        self.rides = rider is not None
        block = 768
        args, specs, groups, begin = [], [], [], 0
        if self.rides:
            args.append(rider)
            specs.append(pl.BlockSpec((8, block), lambda j: (0, jnp.minimum(j, 1))))
        for r in rings:
            number = r.columns // block

            def spec(rows, half, s=begin, n=number):
                return pl.BlockSpec((rows, block), lambda j: (half, jnp.clip(j - s, 0, n - 1)))

            args += [far(r.own), r.from_left, r.from_right, r.right_a, r.left_b]
            specs += [spec(384, 0), spec(192, 1), spec(192, 1), spec(192, 0), spec(192, 0)]
            groups.append((begin, begin + number))
            begin += number
        self.columns = begin * block
        self.rows = 112 if self.rides else 96
        outs = run(
            functools.partial(sum_kernel, groups),
            [place] + args,
            [SMEM] + specs,
            (jax.ShapeDtypeStruct((self.rows, self.columns), BF16),) * 4,
            (pl.BlockSpec((self.rows, block), lambda j: (0, j)),) * 4,
            begin,
            "sum_rings",
            cost(3 * 384 * self.columns, 8 * 384 * self.columns),
            scratch=[pltpu.VMEM((384, block), BF16)],
            after=after,
        )
        self.got = [outs[0]] + [send(outs[d], ring_by(True, d)) for d in (1, 2, 3)]
        self.gate = outs[:1]

    def last(self, after=()):
        block = 1536
        spec = pl.BlockSpec((self.rows, block), lambda j: (0, j))
        riding = (jax.ShapeDtypeStruct((8, D), F32),) if self.rides else ()
        self.keep, away, *ridden = run(
            functools.partial(last_kernel, self.rides),
            [self.place, *self.got],
            [SMEM] + [spec] * 4,
            (
                jax.ShapeDtypeStruct((48, self.columns), F32),
                jax.ShapeDtypeStruct((48, self.columns), BF16),
            )
            + riding,
            (
                pl.BlockSpec((48, block), lambda j: (0, j)),
                pl.BlockSpec((48, block), lambda j: (0, j)),
            )
            + (whole((8, D)),) * len(riding),
            self.columns // block,
            "sum_last",
            cost(4 * 96 * self.columns, 12 * 96 * self.columns),
            scratch=[pltpu.VMEM((96, block), F32)],
            after=after,
        )
        self.arrived = send(away, ZLO)
        if self.rides:
            self.ridden = ridden[0]
        return (away,)


def finish_kernel(*refs):
    ins, (up, down, qkv, out) = refs[:4], refs[4:]
    for layer in range(2):
        keep, arrived = ins[2 * layer : 2 * layer + 2]
        total = keep[...] + arrived[...].astype(F32)
        up[layer] = total[:, :SLICE]
        down[layer] = total[:, SLICE : 2 * SLICE]
        for n in range(3):
            qkv[layer, n] = total[:, 2 * SLICE + n * HID : 2 * SLICE + (n + 1) * HID]
        out[layer] = total[:, 2 * SLICE + 3 * HID :]


def finish(layers):
    shapes = [(2, 48, SLICE), (2, 48, SLICE), (2, 3, 48, HID), (2, 48, HID)]
    columns = layers[0].columns
    return run(
        finish_kernel,
        [a for layer in layers for a in (layer.keep, layer.arrived)],
        [whole((48, columns))] * 4,
        tuple(jax.ShapeDtypeStruct(shape, F32) for shape in shapes),
        tuple(whole(shape) for shape in shapes),
        1,
        "finish",
        cost(96 * columns, 20 * 48 * columns),
    )


def body(tokens, norm_gain, norm_shift, w_qkv, w_out, w_up, w_down, granularity, cotangent):
    zl, y, x, zh, c = (lax.axis_index(a) for a in AXES)
    layers = w_qkv.shape[0]
    core = c.reshape(1).astype(jnp.int32)
    place = jnp.where(c == 0, jnp.stack([x, y, zl, 4, 1]), jnp.stack([y, x, zl, 1, 4]))
    place = place.astype(jnp.int32)
    width = FF // 8 * 2 ** granularity[0, 0] - (zh * 2 + c) * SLICE
    width = width.reshape(1).astype(jnp.int32)
    w_qkv = jnp.transpose(w_qkv, (0, 2, 1, 3))
    low_chip = zh == 0

    positions = jnp.arange(2 * HALF, dtype=F32)[:, None]
    half = E // 2
    frequency = BASE ** (-jnp.arange(half, dtype=F32) / half)
    angles = positions * frequency[None, :]
    cos = jnp.cos(angles)
    sin = jnp.sin(angles)
    cos = jnp.concatenate([cos, cos], axis=1)
    sin = jnp.concatenate([-sin, sin], axis=1)

    def gain(layer, member):
        return norm_gain[layer, member][None, :]

    def shift(layer, member):
        return norm_shift[layer, member][None, :]

    def both_chunks(own):
        other = send(own, FAR)
        return jnp.where(low_chip, own, other), jnp.where(low_chip, other, own)

    def pair(a):
        return lax.all_gather(a, "c", axis=0, tiled=True)

    def core_sum(mine, *theirs):
        other = [lax.dynamic_slice_in_dim(pair(t), (1 - c) * OWN, OWN, 0) for t in theirs]
        return mine.astype(F32) + jnp.concatenate(other, axis=0).astype(F32)

    def exchange(mine, *theirs):
        s = core_sum(mine, *theirs).astype(BF16)
        return s, send(s, FAR)

    stream = list(both_chunks(tokens))
    normed = [pair(norm(stream[k], gain(0, 0), shift(0, 0))) for k in range(2)]
    saved = []
    gate = ()
    sums = [None] * 2
    for layer in range(layers):
        last = layer == layers - 1
        qkv, mixture, hid, slope = ([None] * 2 for _ in range(4))
        mid, normed_two, following = ([None] * 2 for _ in range(3))
        if layer:
            normed = [None] * 2
        for k in range(2):
            if layer:
                stream[k], a = add_norm(mid_before[k], *sums[k], gain(layer, 0), shift(layer, 0), gate)
                normed[k] = pair(a)
            qkv[k], mixture[k], pm, pt = attend(
                layer, k, core, normed[k], w_qkv, w_out, cos, sin, qkv[0], gate
            )
            sums[k] = exchange(pm, pt)
            gate = sums[k][:1]
        keep = {"stream": list(stream), "normed": normed}
        for k in range(2):
            mid[k], a = add_norm(stream[k], *sums[k], gain(layer, 1), shift(layer, 1), gate)
            normed_two[k] = pair(a)
            hid[k], slope[k], pm, pt = feed(layer, width, core, normed_two[k], w_up, w_down, gate)
            if last:
                sums[k] = core_sum(pm, pt)
                gate = (pm,)
            else:
                sums[k] = exchange(pm, pt)
                gate = sums[k][:1]
        mid_before = mid
        keep.update(qkv=qkv, mixture=mixture, mid=mid, normed_two=normed_two, hid=hid, slope=slope)
        saved.append(keep)
    ours = jnp.where(low_chip, sums[0], sums[1])
    away = jnp.where(low_chip, sums[1], sums[0]).astype(BF16)
    base = jnp.where(low_chip, mid[0], mid[1])
    came = send(away, FAR)
    activations = (base + (ours + came.astype(F32))).astype(BF16)

    gradient = both_chunks(cotangent)
    g = [pair(v) for v in gradient]
    norm_sums = [[None, None] for _ in range(layers)]

    def column(j):
        return (0, j)

    def feed_grads(kept, du, g, after):
        number = SLICE // FB
        parts = grads(
            place,
            FB,
            [
                ([far(a) for a in kept["normed_two"]], [(du, (2 * HALF, FB), column)], number),
                (g, [(far(h), (HALF, FB), column) for h in kept["hid"]], number),
            ],
            after,
        )
        return Ring(parts), parts[4:]

    def attend_grads(kept, dqkv, g, after):
        head = (1, 2 * HALF, HID)
        parts = grads(
            place,
            HID,
            [
                ([far(a) for a in kept["normed"]], [(dqkv, head, lambda j: (j, 0, 0))], 3),
                (g, [(far(m), (HALF, HID), lambda j: (0, 0)) for m in kept["mixture"]], 1),
            ],
            after,
        )
        return Ring(parts), parts[4:]

    one, zero = layers - 1, 0
    kept = saved[one]
    du, *parts = feed_back(one, core, *g, w_up, w_down, *kept["slope"], gate)
    s, r = exchange(*parts)
    feed_one, gate = feed_grads(kept, du, g, (s,))
    gradient, low, norm_sums[one][1] = norm_back(kept["mid"], s, r, gradient, gain(one, 1), gate)
    g = [pair(v) for v in low]
    dqkv, *parts = attend_back(one, core, *g, w_qkv, w_out, cos, sin, *kept["qkv"])
    s, r = exchange(*parts)
    gate = feed_one.merge((s,))
    attend_one, gate = attend_grads(kept, dqkv, g, gate)
    gradient, low, norm_sums[one][0] = norm_back(
        kept["stream"], s, r, gradient, gain(one, 0), gate
    )
    g = [pair(v) for v in low]
    kept = saved[zero]
    early = (attend_one.from_left, attend_one.from_right)
    du, *parts = feed_back(zero, core, *g, w_up, w_down, *kept["slope"], early)
    s, r = exchange(*parts)
    gate = attend_one.merge((s,))
    feed_zero, gate = feed_grads(kept, du, g, gate)
    layer_one = Finish(place, [feed_one, attend_one], gate)
    gate = layer_one.gate
    gradient, low, norm_sums[zero][1] = norm_back(
        kept["mid"], s, r, gradient, gain(zero, 1), gate
    )
    g = [pair(v) for v in low]
    dqkv, *parts = attend_back(zero, core, *g, w_qkv, w_out, cos, sin, *kept["qkv"])
    total = core_sum(*parts)
    s = jnp.where(low_chip, total[:OWN], total[OWN:]).astype(BF16)
    away = jnp.where(low_chip, total[OWN:], total[:OWN]).astype(BF16)
    r = send(away, FAR)
    attend_zero, gate = attend_grads(kept, dqkv, g, (away,))
    gate = feed_zero.merge(gate)
    gate = layer_one.last(gate)
    xs = jnp.where(low_chip, *kept["stream"])
    prev = jnp.where(low_chip, *gradient)
    (input_grad,), _, norm_sums[zero][0] = norm_back([xs], s, r, [prev], gain(zero, 0), gate)
    gate = attend_zero.merge((input_grad,))
    half = [0.5 * norm_sums[zero][1], 0.5 * norm_sums[one][0], 0.5 * norm_sums[one][1]]
    sums = jnp.concatenate([norm_sums[zero][0], *half], axis=0)
    sums = sums + send(sums, FAR)
    layer_zero = Finish(place, [feed_zero, attend_zero], (*gate, layer_one.arrived), sums)
    layer_zero.last((came,))
    sums = layer_zero.ridden
    grad_up, grad_down, grad_qkv, grad_out = finish([layer_zero, layer_one])
    one_on, two_on, three_on = (send(sums, ring_by(False, d)) for d in (1, 2, 3))
    sums = (sums + two_on) + (one_on + three_on)
    sums = add_small(sums, send(sums, ZLO), (grad_up,))
    sums = jnp.sum(lax.all_gather(sums, "c", axis=0), axis=0)
    sums = sums.reshape(layers, 2, 2, D)
    gain_grads, shift_grads = sums[:, :, 0], sums[:, :, 1]

    grad_qkv = jnp.transpose(grad_qkv, (0, 2, 1, 3))
    grad_down = jnp.swapaxes(grad_down, 1, 2)
    grad_out = jnp.swapaxes(grad_out, 1, 2)
    return (
        activations,
        input_grad,
        grad_qkv,
        grad_out,
        grad_up,
        grad_down,
        gain_grads,
        shift_grads,
        shift_grads[:, 1, :],
    )


def solution(mesh):
    fine = Mesh(mesh.devices.reshape(SIZES), AXES)
    rows = P(AXES, None)
    dp, tensor = AXES[:3], AXES[3:]
    return jax.shard_map(
        body,
        mesh=fine,
        in_specs=(
            rows,
            P(),
            P(),
            P(None, None, None, tensor),
            P(None, tensor, None),
            P(None, None, tensor),
            P(None, tensor, None),
            P(dp, None),
            rows,
        ),
        out_specs=(
            rows,
            rows,
            P(None, dp, None, tensor),
            P(None, tensor, dp),
            P(None, dp, tensor),
            P(None, tensor, dp),
            P(),
            P(),
            P(),
        ),
        check_vma=False,
    )
```
